512 devices in a mesh: brick: 32 (over x, y_lo, core), slab: 16 (over y_hi, z).
Axes of the slice: x: 4, y: 8 (y_hi: 2, y_lo: 4; y = y_hi * 4 + y_lo), z: 8, core: 2. Of those that a mesh axis runs over, the one named last changes fastest.
Arguments:
- positions: float32 [3, 16, 6144], P(None, 'slab', 'brick'), may hold values from -3 to 3
- types: int32 [16, 6144], P('slab', 'brick'), may hold values from 0 to 1, as said below
- neighbours: int32 [16, 6144, 64], P('slab', 'brick'), may hold values from 0 to 383
- neighbour_count: int32 [16, 6144], P('slab', 'brick'), may hold values from 32 to 64, as said below
- send_index: int32 [16, 6144], P('slab', 'brick'), may hold values from 0 to 191
- cell_x: int32 [16, 6144], P('slab', 'brick'), may hold values from 0 to 7, as said below
- cell_y: int32 [16, 6144], P('slab', 'brick'), may hold values from 0 to 15, as said below
- cell_z: int32 [16, 6144], P('slab', 'brick'), may hold values from 0 to 255, as said below
- spline_fraction: float32 [3, 16, 6144], P(None, 'slab', 'brick'), may hold values from 0 to 1
- embed_first: float32 [2, 25], replicated, may hold values from -4 to 4
- embed_second: float32 [25, 50], replicated, may hold values from -1.25 to 1.25
- embed_third: float32 [50, 100], replicated, may hold values from -0.875 to 0.875
- energy_in: float32 [1600, 240], replicated, may hold values from -0.3125 to 0.3125
- energy_hidden: float32 [2, 240, 240], replicated, may hold values from -0.375 to 0.375
- energy_out: float32 [240], replicated, may hold values from -0.375 to 0.375
- wannier_in: float32 [1600, 240], replicated, may hold values from -0.3125 to 0.3125
- wannier_hidden: float32 [2, 240, 240], replicated, may hold values from -0.375 to 0.375
- wannier_out: float32 [240], replicated, may hold values from -0.01953125 to 0.01953125
- charge_base: float32 [2], replicated, may hold values from -2 to 1
Outputs:
- atom_energy: float32 [16, 6144], P('slab', 'brick')
- potential: float32 [256, 256, 256], P('brick', 'slab')
The draws below stay inside these ranges and needn't reach their ends.
Inputs may be any that keep to these rules, and one draw needn't show every extreme that they name: The first neighbour_count entries of an atom's neighbour row are live, the rest are padding; the first atom of every block has all 64 slots live. `types`: atoms 3k, 3k + 1 and 3k + 2 of a row form one water molecule: one oxygen and two hydrogens. `cell_x`: each hydrogen's first grid point along the first dimension is that of its molecule's oxygen or one further. `cell_y`: each hydrogen's first grid point along the second dimension is that of its molecule's oxygen or one further. `cell_z`: each hydrogen's first grid point along the third dimension is that of its molecule's oxygen or one further.
All inputs are finite; a program needn't handle non-finite values.
Results may differ from the reference program's by a relative error of at most 0.0003.
Values sent between devices are 32-bit elements; how exact they have to be, the bound alone decides.
A program may use at most 64 MiB of HBM per device.

```python
import math
import jax
import jax.numpy as jnp
from jax import lax

NG = 256
A_DEV = 192
NB = 64
EMB1 = 25
EMB2 = 50
EMB3 = 100
AXIS = 16
FIT = 240
FIT_LAYERS = 2
GHOST = 96
CX = 8
CY = 16
ATOMS_B = 6144
DESC = 1600
N_BRICK = 32
N_SLAB = 16


def oxygen_flags(key):
    oxygen_slot = jax.random.randint(key, (N_SLAB, ATOMS_B // 3), 0, 3)
    slot_atom = jnp.repeat(oxygen_slot, 3, axis=1)
    position_in = (jnp.arange(ATOMS_B, dtype=jnp.int32) % 3)[None, :]
    return slot_atom == position_in


def place_cells(key, span, salt):
    oxygen = oxygen_flags(key)
    key = jax.random.fold_in(key, salt)
    anchor_key = jax.random.fold_in(key, 1)
    offset_key = jax.random.fold_in(key, 2)
    anchor = jax.random.randint(anchor_key, (N_SLAB, ATOMS_B // 3), 0, span - 1)
    offset = jax.random.randint(offset_key, (N_SLAB, ATOMS_B), 0, 2)
    column = jnp.arange(ATOMS_B, dtype=jnp.int32)[None, :]
    leading = column % A_DEV < 3
    anchor_atom = jnp.repeat(anchor, 3, axis=1)
    anchor_atom = jnp.where(leading, span - 2, anchor_atom)
    offset = jnp.where(leading, 1, offset)
    return (anchor_atom + jnp.where(oxygen, 0, offset)).astype(jnp.int32)


def draw_types(key, part):
    oxygen = oxygen_flags(key)
    return jnp.where(oxygen, 0, 1).astype(jnp.int32)


def draw_cell_x(key, part):
    return place_cells(key, CX, 11)


def draw_cell_y(key, part):
    return place_cells(key, CY, 13)


def draw_cell_z(key, part):
    return place_cells(key, NG, 17)


def draw_charge_base(key, part):
    key = jax.random.fold_in(key, 21)
    magnitude = jax.random.uniform(key, (), jnp.float32, 1.0, 1.6)
    return jnp.stack([-magnitude, 0.5 * magnitude]).astype(jnp.float32)


def draw_neighbour_count(key, part):
    key = jax.random.fold_in(key, 5)
    counts = jax.random.randint(key, (N_SLAB, ATOMS_B), NB // 2, NB + 1)
    column = jnp.arange(ATOMS_B, dtype=jnp.int32)
    return jnp.where((column % A_DEV == 0)[None, :], NB, counts).astype(jnp.int32)


def touch_ends(drawn, rng, smallest, largest):
    longest = drawn.shape.index(max(drawn.shape))
    spots = []
    for shift in (0, 1):
        where = [jax.random.randint(jax.random.fold_in(rng, axis), (), 0, length) for axis, length in enumerate(drawn.shape)]
        where[longest] = (where[longest] + shift) % drawn.shape[longest]
        spots.append(tuple(where))
    return drawn.at[spots[0]].set(smallest).at[spots[1]].set(largest)


def block_levels(rng, shape, cuts, low, top_value):
    gain, own = 1.0, jax.random.fold_in(rng, 6)
    for position, blocks in cuts:
        steps = jnp.exp(jax.random.uniform(jax.random.fold_in(own, position), (blocks,), jnp.float32, low / len(cuts), top_value / len(cuts)))
        gain = gain * jnp.repeat(steps, shape[position] // blocks).reshape([-1 if axis == position else 1 for axis in range(len(shape))])
    return gain


def noise(key, shape, deviation, most, split=(), held_as=jnp.bfloat16):
    factor_of = block_levels(key, shape, split, -0.22, 0.18) if split else 1.0
    drawn = jax.random.normal(key, shape, jnp.float32) * deviation * factor_of
    return jnp.minimum(jnp.maximum(drawn, -most), most).astype(held_as)


def setup_inputs(seed: int = 0) -> dict:
    streams_of = jax.random.split(jax.random.key(seed), 20)
    return {
        "positions": noise(streams_of[0], (3, N_SLAB, ATOMS_B), 0.5, 3.0, ((1, 16), (2, 32)), jnp.float32),
        "types": draw_types(jax.random.fold_in(streams_of[19], 71), 0),
        "neighbours": touch_ends(jax.random.randint(streams_of[2], (N_SLAB, ATOMS_B, NB), 0, A_DEV + 2 * GHOST), jax.random.fold_in(streams_of[2], 1), 0, (A_DEV + 2 * GHOST) - 1).astype(jnp.int32),
        "neighbour_count": draw_neighbour_count(jax.random.fold_in(streams_of[19], 71), 0),
        "send_index": touch_ends(jax.random.randint(streams_of[4], (N_SLAB, 2 * GHOST * N_BRICK), 0, A_DEV), jax.random.fold_in(streams_of[4], 1), 0, A_DEV - 1).astype(jnp.int32),
        "cell_x": draw_cell_x(jax.random.fold_in(streams_of[19], 71), 0),
        "cell_y": draw_cell_y(jax.random.fold_in(streams_of[19], 71), 0),
        "cell_z": draw_cell_z(jax.random.fold_in(streams_of[19], 71), 0),
        "spline_fraction": jnp.clip(1.0 * jax.random.uniform(streams_of[8], (3, N_SLAB, ATOMS_B), jnp.float32) ** block_levels(streams_of[8], (3, N_SLAB, ATOMS_B), ((1, 16), (2, 32)), -0.2, 0.2), 0.0, 1.0),
        "embed_first": noise(streams_of[9], (2, EMB1), 1.0, 4.0, (), jnp.float32),
        "embed_second": noise(streams_of[10], (EMB1, EMB2), EMB1 ** -0.5, 1.25, (), jnp.float32),
        "embed_third": noise(streams_of[11], (EMB2, EMB3), EMB2 ** -0.5, 0.875, (), jnp.float32),
        "energy_in": noise(streams_of[12], (DESC, FIT), (DESC // 4) ** -0.5, 0.3125, (), jnp.float32),
        "energy_hidden": noise(streams_of[13], (FIT_LAYERS, FIT, FIT), FIT ** -0.5, 0.375, (), jnp.float32),
        "energy_out": noise(streams_of[14], (FIT,), FIT ** -0.5, 0.375, (), jnp.float32),
        "wannier_in": noise(streams_of[15], (DESC, FIT), (DESC // 4) ** -0.5, 0.3125, (), jnp.float32),
        "wannier_hidden": noise(streams_of[16], (FIT_LAYERS, FIT, FIT), FIT ** -0.5, 0.375, (), jnp.float32),
        "wannier_out": noise(streams_of[17], (FIT,), (400 * FIT) ** -0.5, 0.01953125, (), jnp.float32),
        "charge_base": draw_charge_base(jax.random.fold_in(streams_of[19], 71), 0),
    }


HIGH = lax.Precision.HIGHEST


def spline_weights(fraction):
    cubed = fraction * fraction * fraction
    square = fraction * fraction
    return jnp.stack([(1.0 - fraction) * (1.0 - fraction) * (1.0 - fraction) / 6.0,
                      (3.0 * cubed - 6.0 * square + 4.0) / 6.0,
                      (-3.0 * cubed + 3.0 * square + 3.0 * fraction + 1.0) / 6.0,
                      cubed / 6.0])


def fitting(descriptor, weight_in, weight_hidden, weight_out):
    hidden = jnp.tanh(jnp.dot(descriptor, weight_in, precision=HIGH))
    for depth_index in range(weight_hidden.shape[0]):
        hidden = jnp.tanh(jnp.dot(hidden, weight_hidden[depth_index], precision=HIGH)) + hidden
    return jnp.dot(hidden, weight_out, precision=HIGH)


def atom_terms(extended, neighbour_rows, neighbour_total, embed_first, embed_second, embed_third,
               energy_in, energy_hidden, energy_out, wannier_in, wannier_hidden, wannier_out):
    atom_count, slots = neighbour_rows.shape
    ghost_rows = (extended.shape[1] - atom_count) // 2
    block_size = 64 if atom_count % 64 == 0 else atom_count
    blocks = atom_count // block_size
    present = (jnp.arange(slots, dtype=jnp.int32)[None, :] < neighbour_total[:, None]).astype(jnp.float32)
    centre_ids = (ghost_rows + jnp.arange(atom_count, dtype=jnp.int32)).reshape(blocks, block_size)

    def one_block(pieces):
        centre_rows, rows_block, present_block = pieces
        centre_block = extended[:3, centre_rows]
        gathered = extended[:, rows_block]
        offsets = gathered[:3] - centre_block[:, :, None]
        smooth = present_block / (1.0 + jnp.sum(offsets * offsets, axis=0))
        environment = jnp.stack([smooth, smooth * offsets[0], smooth * offsets[1], smooth * offsets[2]], axis=-1)
        kind = gathered[3][:, :, None]
        first = jnp.tanh(smooth[:, :, None] * ((1.0 - kind) * embed_first[0] + kind * embed_first[1]))
        second = jnp.tanh(jnp.einsum('anm,mk->ank', first, embed_second, precision=HIGH)) + jnp.concatenate([first, first], axis=-1)
        third = jnp.tanh(jnp.einsum('anm,mk->ank', second, embed_third, precision=HIGH)) + jnp.concatenate([second, second], axis=-1)
        moments = jnp.einsum('anm,anc->amc', third, environment, precision=HIGH) / slots
        descriptor = jnp.einsum('amc,akc->amk', moments, moments[:, :AXIS], precision=HIGH).reshape(block_size, -1)
        return (fitting(descriptor, energy_in, energy_hidden, energy_out),
                fitting(descriptor, wannier_in, wannier_hidden, wannier_out))

    energy_short, charge_shift = lax.map(one_block, (centre_ids, neighbour_rows.reshape(blocks, block_size, slots),
                                                     present.reshape(blocks, block_size, slots)))
    return energy_short.reshape(atom_count), charge_shift.reshape(atom_count)


def green_table(first, second, third, size):
    def folded(index):
        return jnp.where(index < size // 2, index, index - size).astype(jnp.float32) * (2.0 * math.pi / size)
    kappa_x = folded(first)[:, None, None]
    kappa_y = folded(second)[None, :, None]
    kappa_z = folded(third)[None, None, :]
    squared = kappa_x * kappa_x + kappa_y * kappa_y + kappa_z * kappa_z
    root = ((first[:, None, None] == 0) & (second[None, :, None] == 0) & (third[None, None, :] == 0)).astype(jnp.float32)
    return (1.0 - root) * jnp.exp(-0.5 * squared) / (squared + root)


def reference(positions, types, neighbours, neighbour_count, send_index, cell_x, cell_y, cell_z, spline_fraction,
              embed_first, embed_second, embed_third, energy_in, energy_hidden, energy_out,
              wannier_in, wannier_hidden, wannier_out, charge_base):
    kind_float = types.astype(jnp.float32)
    own_atoms = jnp.concatenate([positions, kind_float[None]], axis=0).reshape(4, N_SLAB, N_BRICK, A_DEV)
    send_rows = send_index.reshape(N_SLAB, N_BRICK, 2 * GHOST)
    outgoing = jnp.take_along_axis(own_atoms, jnp.broadcast_to(send_rows[None], (4,) + send_rows.shape), axis=3)
    lower_ghosts = jnp.roll(outgoing[..., GHOST:], 1, axis=2)
    upper_ghosts = jnp.roll(outgoing[..., :GHOST], -1, axis=2)
    extended = jnp.concatenate([lower_ghosts, own_atoms, upper_ghosts], axis=3)
    total_blocks = N_SLAB * N_BRICK
    extended_blocks = jnp.moveaxis(extended, 0, 2).reshape(total_blocks, 4, A_DEV + 2 * GHOST)
    neighbour_blocks = neighbours.reshape(total_blocks, A_DEV, NB)
    count_blocks = neighbour_count.reshape(total_blocks, A_DEV)

    def per_block(pieces):
        return atom_terms(pieces[0], pieces[1], pieces[2], embed_first, embed_second, embed_third,
                          energy_in, energy_hidden, energy_out, wannier_in, wannier_hidden, wannier_out)

    energy_short, charge_shift = lax.map(per_block, (extended_blocks, neighbour_blocks, count_blocks))
    energy_short = energy_short.reshape(N_SLAB, ATOMS_B)
    charge = (1.0 - kind_float) * charge_base[0] + kind_float * charge_base[1] + charge_shift.reshape(N_SLAB, ATOMS_B)

    brick_column = (jnp.arange(ATOMS_B, dtype=jnp.int32) // A_DEV)[None, :]
    slab_row = jnp.arange(N_SLAB, dtype=jnp.int32)[:, None]
    steps_four = jnp.arange(4, dtype=jnp.int32)[:, None, None]
    index_x = (brick_column * CX + cell_x + steps_four) % NG
    index_y = (slab_row * CY + cell_y + steps_four) % NG
    index_z = (cell_z + steps_four) % NG
    weight_x = spline_weights(spline_fraction[0])
    weight_y = spline_weights(spline_fraction[1])
    weight_z = spline_weights(spline_fraction[2])
    shape_all = (4, 4, 4, N_SLAB, ATOMS_B)
    point_x = jnp.broadcast_to(index_x[:, None, None], shape_all)
    point_y = jnp.broadcast_to(index_y[None, :, None], shape_all)
    point_z = jnp.broadcast_to(index_z[None, None, :], shape_all)
    product = weight_x[:, None, None] * weight_y[None, :, None] * weight_z[None, None, :]
    charge_grid = jnp.zeros((NG, NG, NG), jnp.float32).at[point_x, point_y, point_z].add(product * charge)
    spectrum = jnp.fft.fftn(charge_grid)
    grid_index = jnp.arange(NG, dtype=jnp.int32)
    factor = green_table(grid_index, grid_index, grid_index, NG)
    potential = jnp.real(jnp.fft.ifftn(spectrum * factor)).astype(jnp.float32)
    potential_at = jnp.sum(potential[point_x, point_y, point_z] * product, axis=(0, 1, 2))
    atom_energy = energy_short + 0.5 * charge * potential_at
    return atom_energy, potential
```

```python
import math

import jax
import jax.numpy as jnp
import numpy as np
from jax import lax
from jax.experimental import pallas as pl
from jax.experimental.pallas import tpu as pltpu
from jax.sharding import PartitionSpec as P

NG = 256
A = 192
NB = 32
NS = 16
CX = 8
CY = 16
WX = 11
WY = 24
MIB = 1024 * 1024
F32 = jnp.float32
BF16 = jnp.bfloat16
HIGH = lax.Precision.HIGH
HIGHEST = lax.Precision.HIGHEST
MESH = pl.DeviceIdType.MESH

NN = (((1,), (0,)), ((), ()))
NT = (((1,), (1,)), ((), ()))


def split(table):
    table = np.asarray(table, np.float64)
    high = np.asarray(table, np.float32).astype(jnp.bfloat16)
    low = (table - high.astype(np.float64)).astype(np.float32).astype(jnp.bfloat16)
    return high, low


def real_basis():
    n = np.arange(NG)[:, None]
    j = np.arange(NG)[None, :]
    phase = 2.0 * np.pi * ((n * j) % NG) / NG
    basis = np.where(j <= NG // 2, np.cos(phase), np.sin(phase)) * math.sqrt(2.0 / NG)
    basis[:, 0] = 1.0 / 16.0
    basis[:, NG // 2] = np.where(np.arange(NG) % 2 == 0, 1.0, -1.0) / 16.0
    return basis


def transform_tables():
    basis = real_basis()
    slab, offset = np.divmod(np.arange(NS * WY), WY)
    window = basis[(slab * CY + offset) % NG] * (offset < CY + 3)[:, None]
    b = np.arange(NB)
    angle = 2.0 * np.pi * np.outer(b, b) / NB
    eye8 = np.eye(8)
    cos_b = np.kron(np.cos(angle), eye8)
    sin_b = np.kron(np.sin(angle), eye8)
    left = np.concatenate([cos_b, sin_b], axis=0)
    left_back = np.concatenate([cos_b, -sin_b], axis=1)
    xw = np.arange(16)
    live = (xw < WX)[:, None]
    small = 2.0 * np.pi * np.outer(xw, np.arange(8)) / 8
    eye16 = np.eye(16)
    cos_m = np.kron(np.cos(small) * live, eye16)
    sin_m = np.kron(np.sin(small) * live, eye16)
    right = np.block([[cos_m, -sin_m], [sin_m, cos_m]])
    right_back = np.block([[cos_m.T, sin_m.T], [-sin_m.T, cos_m.T]])
    kb = np.repeat(b, 8)[:, None]
    lane_x = np.repeat(xw, 16)[None, :]
    twist = 2.0 * np.pi * kb * lane_x / NG
    return {
        "y": split(window.T),
        "y_back": split(window),
        "left": split(left),
        "left_back": split(left_back),
        "right": split(right),
        "right_back": split(right_back),
        "twist": (np.cos(twist).astype(np.float32), np.sin(twist).astype(np.float32)),
        "z": split(basis),
        "z_back": split(basis.T),
    }


def second_rows():
    rows = list(range(24)) + list(range(25, 49)) + [24, 49, 24, 49]
    return rows


def third_rows():
    second = second_rows()
    return [f for f in second[:48]] + [50 + f for f in second[:48]] + [24, 49, 74, 99]


def one_hot(rows, height, width):
    table = np.zeros((height, width), np.float32)
    for row, feature in enumerate(rows):
        table[row, feature] = 1.0
    return table


def embedding_tables():
    first = one_hot(list(range(25)) + [24, 24, 24], 32, 25)
    second = one_hot(second_rows(), 64, 50)
    third = one_hot(third_rows(), 112, 100)
    columns_first = np.tile(np.eye(25, 32, dtype=np.float32), (1, 3))
    placed = np.zeros((50, 64), np.float32)
    for row, feature in enumerate(second_rows()[:50]):
        placed[feature, row] = 1.0
    columns_second = np.tile(placed, (1, 3))
    place = np.zeros(104, np.int32)
    for row, feature in enumerate(third_rows()):
        place[feature] = row
    lanes = np.arange(13 * 128) // 16
    spread = place[lanes].reshape(13, 128).astype(np.int32)
    spread = np.concatenate([spread, np.zeros((3, 128), np.int32)])
    return first, second, third, columns_first, columns_second, spread


def halves(values):
    high = values.astype(BF16)
    low = (values - high.astype(F32)).astype(BF16)
    return high, low


def dot(a, b, dims=NN):
    return lax.dot_general(a, b, dims, preferred_element_type=F32)


def dot3(a, b, dims=NN):
    return dot(a[0], b[0], dims) + (dot(a[0], b[1], dims) + dot(a[1], b[0], dims))


def lanes_iota(shape):
    return lax.broadcasted_iota(jnp.int32, shape, 1)


def rows_iota(shape):
    return lax.broadcasted_iota(jnp.int32, shape, 0)


def pick(row, index):
    table = jnp.broadcast_to(row, index.shape)
    return jnp.take_along_axis(table, index, axis=1, mode="promise_in_bounds")


def spline_rows(u):
    cubed = u * u * u
    square = u * u
    rest = 1.0 - u
    return (
        rest * rest * rest / 6.0,
        (3.0 * cubed - 6.0 * square + 4.0) / 6.0,
        (-3.0 * cubed + 3.0 * square + 3.0 * u + 1.0) / 6.0,
        cubed / 6.0,
    )


def place_rows(start, weights, height, wrap):
    offset = rows_iota((height, A)) - start
    if wrap:
        offset = offset & (wrap - 1)
    result = jnp.zeros((height, A), F32)
    for step in range(4):
        result = jnp.where(offset == step, weights[step], result)
    return result


def spreads(cx_ref, cy_ref, cz_ref, frac_ref):
    wx = place_rows(cx_ref[...], spline_rows(frac_ref[0]), 16, 0)
    wy = place_rows(cy_ref[...], spline_rows(frac_ref[1]), WY, 0)
    wz = place_rows(cz_ref[...], spline_rows(frac_ref[2]), NG, NG)
    wxy = jnp.concatenate([wx[x : x + 1] * wy for x in range(WX)], axis=0)
    return wxy, wz


def atoms_kernel(
    own_ref, low_ref, upp_ref, count_ref, neigh_ref,
    cx_ref, cy_ref, cz_ref, frac_ref,
    first_ref, second_ref, third_ref,
    e_in_ref, e_hid_ref, e_out_ref, w_in_ref, w_hid_ref, w_out_ref, base_ref,
    p1_ref, p2_ref, p3_ref, c1_ref, c2_ref, spread_ref, zh_ref, zl_ref,
    scal_ref, send_ref,
    env_ref, moment_ref, desc_h_ref, desc_l_ref, w2_ref, w3_ref,
):
    f1 = lax.dot_general(p1_ref[...], first_ref[...], NT, precision=HIGHEST)
    oxygen, hydrogen = f1[:, 0:1], f1[:, 1:2]
    w2 = lax.dot_general(p2_ref[...], second_ref[...], NT, precision=HIGHEST)
    w2 = lax.dot_general(w2, c1_ref[...], NN, precision=HIGHEST)
    high, low = halves(w2)
    slot = lanes_iota((64, 96)) // 32
    w2_ref[...] = jnp.where(slot == 1, low.astype(F32), high.astype(F32)).astype(BF16)
    w3 = lax.dot_general(p3_ref[...], third_ref[...], NT, precision=HIGHEST)
    w3 = lax.dot_general(w3, c2_ref[...], NN, precision=HIGHEST)
    high, low = halves(w3)
    slot = lanes_iota((112, 192)) // 64
    w3_ref[...] = jnp.where(slot == 1, low.astype(F32), high.astype(F32)).astype(BF16)

    n = jnp.concatenate([neigh_ref[0, 0:96, :], neigh_ref[0, 96:192, :]], axis=1)
    low_index = pick_index = (n - 96) & 127
    lower_index = n & 127
    upper_index = (n - 288) & 127
    lane = lanes_iota((96, 128))
    centre = rows_iota((96, 128)) + jnp.where(lane >= 64, 96, 0)
    centre_index = centre & 127
    ghosts_low = jnp.broadcast_to(low_ref[5:6, 0:128], (8, 128)).astype(jnp.int32)
    ghosts_upp = jnp.broadcast_to(upp_ref[4:5, 0:128], (8, 128)).astype(jnp.int32)

    def ghost_rows(ref, index):
        near = jnp.take_along_axis(ref[:, 0:128], index & 127, axis=1, mode="promise_in_bounds")
        far = jnp.take_along_axis(ref[:, 128:256], index & 127, axis=1, mode="promise_in_bounds")
        return jnp.where(index < 128, near, far)

    lower = ghost_rows(low_ref, ghosts_low)
    upper = ghost_rows(upp_ref, ghosts_upp)
    gathered = []
    for c in range(4):
        value = pick(own_ref[c : c + 1, 0:128], pick_index)
        value = jnp.where(n < 224, value, pick(own_ref[c : c + 1, 128:256], pick_index))
        value = jnp.where(n < 96, pick(lower[c : c + 1], lower_index), value)
        value = jnp.where(n >= 288, pick(upper[c : c + 1], upper_index), value)
        gathered.append(value)
    offsets = []
    for c in range(3):
        here = jnp.where(
            centre < 128,
            pick(own_ref[c : c + 1, 0:128], centre_index),
            pick(own_ref[c : c + 1, 128:256], centre_index),
        )
        offsets.append(gathered[c] - here)
    total = jnp.where(
        centre < 128,
        pick(count_ref[0:1, 0:128], centre_index),
        pick(count_ref[0:1, 128:256], centre_index),
    )
    squared = offsets[0] * offsets[0] + offsets[1] * offsets[1] + offsets[2] * offsets[2]
    smooth = jnp.where((lane & 63).astype(F32) < total, 1.0 / (1.0 + squared), 0.0)
    env_ref[0] = smooth
    for c in range(3):
        env_ref[c + 1] = smooth * offsets[c]
    env_ref[4] = gathered[3]

    oxygen_wide = jnp.broadcast_to(oxygen, (32, 128))
    hydrogen_wide = jnp.broadcast_to(hydrogen, (32, 128))
    row8 = rows_iota((8, 128))
    left8 = lanes_iota((8, 128)) < 64

    def chunk(step, carry):
        at = pl.multiple_of(step * 8, 8)
        first = []
        for r in range(8):
            sm = env_ref[0, pl.ds(at + r, 1), :]
            kind = env_ref[4, pl.ds(at + r, 1), :]
            mixing = jnp.where(kind > 0.5, hydrogen_wide, oxygen_wide)
            first.append(jnp.tanh(sm * mixing))
        first = jnp.concatenate(first, axis=1)
        high, low = halves(first)
        second = dot(w2_ref[...], jnp.concatenate([high, high, low], axis=0))
        second = jnp.tanh(second[:56]) + jnp.concatenate([first[:24], first], axis=0)
        padded = jnp.concatenate([second, jnp.zeros((8, 1024), F32)], axis=0)
        high, low = halves(padded)
        third = dot(w3_ref[...], jnp.concatenate([high, high, low], axis=0))
        third = jnp.tanh(third[:104]) + jnp.concatenate([second[:48], second], axis=0)
        third = jnp.concatenate([third, jnp.zeros((8, 1024), F32)], axis=0)
        third = halves(third)
        rows = []
        for c in range(4):
            value = env_ref[c, pl.ds(at, 8), :] * (1.0 / 64.0)
            for half in range(2):
                side = left8 if half == 0 else jnp.logical_not(left8)
                kept = jnp.where(side, value, 0.0)
                rows.append(
                    jnp.concatenate([jnp.where(row8 == r, kept, 0.0) for r in range(8)], axis=1)
                )
        rows = halves(jnp.concatenate(rows, axis=0))
        both = dot(jnp.concatenate(rows, axis=0), third[0], NT)
        moments = both[:64] + both[64:] + dot(rows[0], third[1], NT)
        for c in range(4):
            for half in range(2):
                k = (c * 2 + half) * 8
                moment_ref[c, pl.ds(at + half * 96, 8), 0:112] = moments[k : k + 8]
        return carry

    lax.fori_loop(0, 12, chunk, 0)

    lane_a = lanes_iota((A, 128))
    moments = [jnp.where(lane_a < 104, moment_ref[c], 0.0) for c in range(4)]
    factors = [
        jnp.take_along_axis(m, lane_a & 15, axis=1, mode="promise_in_bounds") for m in moments
    ]
    for j in range(13):
        index = jnp.broadcast_to(spread_ref[j : j + 1, :], (A, 128))
        value = None
        for c in range(4):
            term = jnp.take_along_axis(moments[c], index, axis=1, mode="promise_in_bounds")
            term = term * factors[c]
            value = term if value is None else value + term
        high, low = halves(value)
        desc_h_ref[:, j * 128 : (j + 1) * 128] = high
        desc_l_ref[:, j * 128 : (j + 1) * 128] = low

    def network(in_ref, hid_ref, out_ref):
        weight = halves(in_ref[...])
        hidden = jnp.tanh(dot3((desc_h_ref[:, 0:1600], desc_l_ref[:, 0:1600]), weight))
        for layer in range(2):
            hidden = jnp.tanh(dot3(halves(hidden), halves(hid_ref[layer]))) + hidden
        row = jnp.broadcast_to(out_ref[...], (16, 240))
        return dot3(halves(row), halves(hidden), NT)[0:1]

    energy = network(e_in_ref, e_hid_ref, e_out_ref)
    shift = network(w_in_ref, w_hid_ref, w_out_ref)
    charge = jnp.where(own_ref[3:4, 0:A] > 0.5, base_ref[1], base_ref[0]) + shift
    scal_ref[...] = jnp.concatenate([energy, charge, jnp.zeros((6, A), F32)], axis=0)

    wxy, wz = spreads(cx_ref, cy_ref, cz_ref, frac_ref)
    grid = dot3(halves(wxy), halves(wz * charge), NT)
    spectrum = dot3(halves(grid), (zh_ref[...], zl_ref[...]))
    chunk_lane = lanes_iota((WY, 128)) // 16
    for s in range(NS):
        tile, chunk_from = divmod(s, 8)
        for half in range(2):
            out = jnp.zeros((WY, 128), F32)
            for x in range(8 * half, min(8 * half + 8, WX)):
                source = spectrum[x * WY : (x + 1) * WY, tile * 128 : (tile + 1) * 128]
                shift_by = 16 * (x % 8 - chunk_from) % 128
                if shift_by:
                    source = pltpu.roll(source, shift_by, 1)
                out = jnp.where(chunk_lane == x % 8, source, out)
            send_ref[s, :, half * 128 : (half + 1) * 128] = out


def solve_kernel(
    send_ref, yh_ref, yl_ref, lh_ref, ll_ref, rh_ref, rl_ref, tc_ref, ts_ref,
    rbh_ref, rbl_ref, lbh_ref, lbl_ref, ybh_ref, ybl_ref,
    out_ref,
    in1, out2, in2, out3, in3, out4,
    send1, recv1, send2, recv2, send3, recv3, send4, recv4,
):
    b = lax.axis_index("brick")
    s = lax.axis_index("slab")

    barrier = pltpu.get_barrier_semaphore()

    def greet_slab(i, carry):
        pl.semaphore_signal(barrier, inc=1, device_id=(b, lax.rem(s + i, NS)), device_id_type=MESH)
        return carry

    def greet_brick(i, carry):
        pl.semaphore_signal(barrier, inc=1, device_id=(lax.rem(b + i, NB), s), device_id_type=MESH)
        return carry

    lax.fori_loop(1, NS, greet_slab, 0)
    lax.fori_loop(1, NB, greet_brick, 0)
    pl.semaphore_wait(barrier, NS + NB - 2)

    def over_slab(source, target, send_sem, recv_sem):
        def copy(i):
            to = lax.rem(s + i, NS)
            return pltpu.make_async_remote_copy(
                src_ref=source.at[to],
                dst_ref=target.at[s],
                send_sem=send_sem.at[to],
                recv_sem=recv_sem.at[s],
                device_id=(b, to),
                device_id_type=MESH,
            )

        def arrival(i):
            frm = lax.rem(s + i, NS)
            return pltpu.make_async_remote_copy(
                src_ref=source.at[frm],
                dst_ref=target.at[frm],
                send_sem=send_sem.at[frm],
                recv_sem=recv_sem.at[frm],
                device_id=(b, frm),
                device_id_type=MESH,
            )

        def start(i, carry):
            copy(i).start()
            return carry

        def wait(i, carry):
            arrival(i).wait_recv()
            return carry

        def drain(i, carry):
            copy(i).wait_send()
            return carry

        lax.fori_loop(1, NS, start, 0)
        target[s] = source[s]
        lax.fori_loop(1, NS, wait, 0)
        return lambda: lax.fori_loop(1, NS, drain, 0)

    def over_brick(source, target, send_sem, recv_sem):
        def copy(i):
            to = lax.rem(b + i, NB)
            return pltpu.make_async_remote_copy(
                src_ref=source.at[to],
                dst_ref=target.at[b],
                send_sem=send_sem.at[to],
                recv_sem=recv_sem.at[b],
                device_id=(to, s),
                device_id_type=MESH,
            )

        def arrival(i):
            frm = lax.rem(b + i, NB)
            return pltpu.make_async_remote_copy(
                src_ref=source.at[frm],
                dst_ref=target.at[frm],
                send_sem=send_sem.at[frm],
                recv_sem=recv_sem.at[frm],
                device_id=(frm, s),
                device_id_type=MESH,
            )

        def start(i, carry):
            copy(i).start()
            return carry

        def wait(i, carry):
            arrival(i).wait_recv()
            return carry

        def drain(i, carry):
            copy(i).wait_send()
            return carry

        lax.fori_loop(1, NB, start, 0)
        target[b] = source[b]
        lax.fori_loop(1, NB, wait, 0)
        return lambda: lax.fori_loop(1, NB, drain, 0)

    drain1 = over_slab(send_ref, in1, send1, recv1)
    data = halves(in1[...].reshape(NS * WY, NG))
    out2[...] = dot3((yh_ref[...], yl_ref[...]), data).reshape(NB, 8, NG)
    drain2 = over_brick(out2, in2, send2, recv2)

    row = rows_iota((256, 128))
    lane = lanes_iota((256, 128))

    def kappa(index):
        folded = jnp.minimum(index, NG - index)
        return folded.astype(F32) * (2.0 * math.pi / NG)

    kx = kappa(row // 8 + 32 * (lane // 16))
    ky = kappa(b * 8 + row % 8)
    kz = kappa(s * 16 + lane % 16)
    squared = kx * kx + ky * ky + kz * kz
    root = jnp.where(squared == 0.0, 1.0, 0.0)
    green = (1.0 - root) * jnp.exp(-0.5 * squared) / (squared + root) * (1.0 / NG)
    green = jnp.concatenate([green, green], axis=1)

    data = halves(in2[...].reshape(256, NG))
    both = dot3((lh_ref[...], ll_ref[...]), data)
    uc, us = both[:256], both[256:]
    tc, ts = tc_ref[...], ts_ref[...]
    turned = jnp.concatenate([uc * tc - us * ts, -(uc * ts + us * tc)], axis=1)
    modes = dot3(halves(turned), (rh_ref[...], rl_ref[...])) * green
    back = dot3(halves(modes), (rbh_ref[...], rbl_ref[...]))
    vr, vi = back[:, :256], back[:, 256:]
    turned = jnp.concatenate([vr * tc - vi * ts, vr * ts + vi * tc], axis=0)
    out3[...] = dot3((lbh_ref[...], lbl_ref[...]), halves(turned)).reshape(NB, 8, NG)
    drain3 = over_brick(out3, in3, send3, recv3)
    data = halves(in3[...].reshape(256, NG))
    out4[...] = dot3((ybh_ref[...], ybl_ref[...]), data).reshape(NS, WY, NG)
    drain4 = over_slab(out4, out_ref, send4, recv4)
    drain1()
    drain2()
    drain3()
    drain4()


def sample_kernel(
    in_ref, cx_ref, cy_ref, cz_ref, frac_ref, scal_ref, zh_ref, zl_ref, energy_ref, pot_ref, modes_ref
):
    chunk_lane = lanes_iota((WY, 128)) // 16
    for x in range(WX):
        half, chunk_from = divmod(x, 8)
        for tile in range(2):
            out = jnp.zeros((WY, 128), F32)
            for c in range(8):
                source = in_ref[8 * tile + c, :, half * 128 : (half + 1) * 128]
                shift_by = 16 * (c - chunk_from) % 128
                if shift_by:
                    source = pltpu.roll(source, shift_by, 1)
                out = jnp.where(chunk_lane == c, source, out)
            modes_ref[x * WY : (x + 1) * WY, tile * 128 : (tile + 1) * 128] = out
    potential = dot3(halves(modes_ref[...]), (zh_ref[...], zl_ref[...]))
    for x in range(CX):
        pot_ref[x] = potential[x * WY : x * WY + CY]
    wxy, wz = spreads(cx_ref, cy_ref, cz_ref, frac_ref)
    sampled = dot3(halves(potential), halves(wz))
    at = jnp.sum(sampled * wxy, axis=0, keepdims=True)
    energy_ref[...] = scal_ref[0:1, :] + 0.5 * scal_ref[1:2, :] * at


VMEM = pl.BlockSpec(memory_space=pltpu.VMEM)
SMEM = pl.BlockSpec(memory_space=pltpu.SMEM)


def per_device(
    positions, types, neighbours, neighbour_count, send_index, cell_x, cell_y, cell_z, spline_fraction,
    embed_first, embed_second, embed_third, energy_in, energy_hidden, energy_out,
    wannier_in, wannier_hidden, wannier_out, charge_base,
):
    tables = transform_tables()
    embedding = embedding_tables()

    def wide(rows):
        return jnp.pad(rows, ((0, 0), (0, 256 - rows.shape[1])))

    own = jnp.concatenate(
        [
            wide(positions[:, 0]),
            wide(types.astype(F32)),
            wide(send_index[:, :96].astype(F32)),
            wide(send_index[:, 96:].astype(F32)),
            jnp.zeros((2, 256), F32),
        ],
        axis=0,
    )
    lower = lax.ppermute(own, "brick", [(i, (i + 1) % NB) for i in range(NB)])
    upper = lax.ppermute(own, "brick", [((i + 1) % NB, i) for i in range(NB)])
    count = wide(neighbour_count.astype(F32))

    scalars, send = pl.pallas_call(
        atoms_kernel,
        out_shape=(
            jax.ShapeDtypeStruct((8, A), F32),
            jax.ShapeDtypeStruct((NS, WY, NG), F32),
        ),
        in_specs=[VMEM] * 18 + [SMEM] + [VMEM] * 8,
        out_specs=(VMEM, VMEM),
        scratch_shapes=[
            pltpu.VMEM((5, 96, 128), F32),
            pltpu.VMEM((4, A, 128), F32),
            pltpu.VMEM((A, 1664), BF16),
            pltpu.VMEM((A, 1664), BF16),
            pltpu.VMEM((64, 96), BF16),
            pltpu.VMEM((112, 192), BF16),
        ],
        compiler_params=pltpu.CompilerParams(vmem_limit_bytes=48 * MIB),
        name="atoms",
    )(
        own, lower, upper, count, neighbours,
        cell_x, cell_y, cell_z, spline_fraction,
        embed_first, embed_second, embed_third,
        energy_in, energy_hidden, energy_out.reshape(1, -1),
        wannier_in, wannier_hidden, wannier_out.reshape(1, -1), charge_base,
        *embedding, *tables["z"],
    )

    received = pl.pallas_call(
        solve_kernel,
        out_shape=jax.ShapeDtypeStruct((NS, WY, NG), F32),
        in_specs=[VMEM] * 15,
        out_specs=VMEM,
        scratch_shapes=[
            pltpu.VMEM((NS, WY, NG), F32),
            pltpu.VMEM((NB, 8, NG), F32),
            pltpu.VMEM((NB, 8, NG), F32),
            pltpu.VMEM((NB, 8, NG), F32),
            pltpu.VMEM((NB, 8, NG), F32),
            pltpu.VMEM((NS, WY, NG), F32),
            pltpu.SemaphoreType.DMA((NS,)),
            pltpu.SemaphoreType.DMA((NS,)),
            pltpu.SemaphoreType.DMA((NB,)),
            pltpu.SemaphoreType.DMA((NB,)),
            pltpu.SemaphoreType.DMA((NB,)),
            pltpu.SemaphoreType.DMA((NB,)),
            pltpu.SemaphoreType.DMA((NS,)),
            pltpu.SemaphoreType.DMA((NS,)),
        ],
        compiler_params=pltpu.CompilerParams(
            collective_id=1, has_side_effects=True, vmem_limit_bytes=40 * MIB
        ),
        name="solve",
    )(
        send, *tables["y"], *tables["left"], *tables["right"], *tables["twist"],
        *tables["right_back"], *tables["left_back"], *tables["y_back"],
    )

    energy, potential = pl.pallas_call(
        sample_kernel,
        out_shape=(
            jax.ShapeDtypeStruct((1, A), F32),
            jax.ShapeDtypeStruct((CX, CY, NG), F32),
        ),
        in_specs=[VMEM] * 8,
        out_specs=(VMEM, VMEM),
        scratch_shapes=[pltpu.VMEM((WX * WY, NG), F32)],
        compiler_params=pltpu.CompilerParams(vmem_limit_bytes=40 * MIB),
        name="sample",
    )(received, cell_x, cell_y, cell_z, spline_fraction, scalars, *tables["z_back"])
    return energy, potential


def solution(mesh):
    row = P("slab", "brick")
    three = P(None, "slab", "brick")
    placed = (three, row, P("slab", "brick", None), row, row, row, row, row, three) + (P(),) * 10
    return jax.shard_map(
        per_device,
        mesh=mesh,
        in_specs=placed,
        out_specs=(row, P("brick", "slab", None)),
        check_vma=False,
    )
```

```python
import math

import jax
import jax.numpy as jnp
import numpy as np
from jax import lax
from jax.experimental import pallas as pl
from jax.experimental.pallas import tpu as pltpu
from jax.sharding import PartitionSpec as P

NG = 256
A = 192
NB = 32
NS = 16
CX = 8
CY = 16
WX = 11
WY = 24
MIB = 1024 * 1024
F32 = jnp.float32
BF16 = jnp.bfloat16
HIGH = lax.Precision.HIGH
HIGHEST = lax.Precision.HIGHEST
MESH = pl.DeviceIdType.MESH

NN = (((1,), (0,)), ((), ()))
NT = (((1,), (1,)), ((), ()))


def split(table):
    table = np.asarray(table, np.float64)
    high = np.asarray(table, np.float32).astype(jnp.bfloat16)
    low = (table - high.astype(np.float64)).astype(np.float32).astype(jnp.bfloat16)
    return high, low


def real_basis():
    n = np.arange(NG)[:, None]
    j = np.arange(NG)[None, :]
    phase = 2.0 * np.pi * ((n * j) % NG) / NG
    basis = np.where(j <= NG // 2, np.cos(phase), np.sin(phase)) * math.sqrt(2.0 / NG)
    basis[:, 0] = 1.0 / 16.0
    basis[:, NG // 2] = np.where(np.arange(NG) % 2 == 0, 1.0, -1.0) / 16.0
    return basis


def transform_tables():
    basis = real_basis()
    slab, offset = np.divmod(np.arange(NS * WY), WY)
    window = basis[(slab * CY + offset) % NG] * (offset < CY + 3)[:, None]
    b = np.arange(NB)
    angle = 2.0 * np.pi * np.outer(b, b) / NB
    eye8 = np.eye(8)
    cos_b = np.kron(np.cos(angle), eye8)
    sin_b = np.kron(np.sin(angle), eye8)
    left = np.concatenate([cos_b, sin_b], axis=0)
    left_back = np.concatenate([cos_b, -sin_b], axis=1)
    xw = np.arange(16)
    live = (xw < WX)[:, None]
    small = 2.0 * np.pi * np.outer(xw, np.arange(8)) / 8
    eye16 = np.eye(16)
    cos_m = np.kron(np.cos(small) * live, eye16)
    sin_m = np.kron(np.sin(small) * live, eye16)
    right = np.block([[cos_m, -sin_m], [sin_m, cos_m]])
    right_back = np.block([[cos_m.T, sin_m.T], [-sin_m.T, cos_m.T]])
    kb = np.repeat(b, 8)[:, None]
    lane_x = np.repeat(xw, 16)[None, :]
    twist = 2.0 * np.pi * kb * lane_x / NG
    return {
        "y": split(window.T),
        "y_back": split(window),
        "left": split(left),
        "left_back": split(left_back),
        "right": split(right),
        "right_back": split(right_back),
        "twist": (np.cos(twist).astype(np.float32), np.sin(twist).astype(np.float32)),
        "z": split(basis),
        "z_back": split(basis.T),
    }


def second_rows():
    rows = list(range(24)) + list(range(25, 49)) + [24, 49, 24, 49]
    return rows


def third_rows():
    second = second_rows()
    return [f for f in second[:48]] + [50 + f for f in second[:48]] + [24, 49, 74, 99]


def one_hot(rows, height, width):
    table = np.zeros((height, width), np.float32)
    for row, feature in enumerate(rows):
        table[row, feature] = 1.0
    return table


def embedding_tables():
    first = one_hot(list(range(25)) + [24, 24, 24], 32, 25)
    second = one_hot(second_rows(), 64, 50)
    third = one_hot(third_rows(), 112, 100)
    columns_first = np.tile(np.eye(25, 32, dtype=np.float32), (1, 3))
    placed = np.zeros((50, 64), np.float32)
    for row, feature in enumerate(second_rows()[:50]):
        placed[feature, row] = 1.0
    columns_second = np.tile(placed, (1, 3))
    table = np.zeros((296, 256), np.float32)
    table[0:32, :25] = first
    table[32:96, :50] = second
    table[96:208, :100] = third
    table[208:233, :96] = columns_first
    table[240:290, :192] = columns_second
    return table


def places():
    rows = third_rows()
    return [rows.index(feature) for feature in range(100)]


def halves(values):
    high = values.astype(BF16)
    low = (values - high.astype(F32)).astype(BF16)
    return high, low


def dot(a, b, dims=NN):
    return lax.dot_general(a, b, dims, preferred_element_type=F32)


def dot3(a, b, dims=NN):
    return dot(a[0], b[0], dims) + (dot(a[0], b[1], dims) + dot(a[1], b[0], dims))


def lanes_iota(shape):
    return lax.broadcasted_iota(jnp.int32, shape, 1)


def rows_iota(shape):
    return lax.broadcasted_iota(jnp.int32, shape, 0)


def pick(row, index):
    table = jnp.broadcast_to(row, index.shape)
    return jnp.take_along_axis(table, index, axis=1, mode="promise_in_bounds")


def spline_rows(u):
    cubed = u * u * u
    square = u * u
    rest = 1.0 - u
    return (
        rest * rest * rest / 6.0,
        (3.0 * cubed - 6.0 * square + 4.0) / 6.0,
        (-3.0 * cubed + 3.0 * square + 3.0 * u + 1.0) / 6.0,
        cubed / 6.0,
    )


def place_rows(start, weights, height, wrap):
    offset = rows_iota((height, A)) - start
    if wrap:
        offset = offset & (wrap - 1)
    result = jnp.zeros((height, A), F32)
    for step in range(4):
        result = jnp.where(offset == step, weights[step], result)
    return result


def spreads(cx_ref, cy_ref, cz_ref, frac_ref):
    wx = place_rows(cx_ref[...], spline_rows(frac_ref[0]), 16, 0)
    wy = place_rows(cy_ref[...], spline_rows(frac_ref[1]), WY, 0)
    wz = place_rows(cz_ref[...], spline_rows(frac_ref[2]), NG, NG)
    wxy = jnp.concatenate([wx[x : x + 1] * wy for x in range(WX)], axis=0)
    return wxy, wz


LOADED = 20


def atoms_kernel(
    pos_any, typ_any, snd_any, neigh_any, count_any, cx_any, cy_any, cz_any, frac_any,
    first_any, second_any, third_any, e_in_any, e_hid_any, e_out_any, w_in_any, w_hid_any, w_out_any,
    base_any, table_any, z_any,
    scal_ref, send_ref,
    pos_ref, typ_ref, neigh_ref, count_ref, cx_ref, cy_ref, cz_ref, frac_ref,
    first_ref, second_ref, third_ref, e_in_ref, e_hid_ref, e_out_ref, w_in_ref, w_hid_ref, w_out_ref,
    base_ref, table_ref, z_ref,
    low_pos, low_typ, low_snd, upp_pos, upp_typ, upp_snd,
    env_ref, moment_ref, in_h_ref, in_l_ref, desc_h_ref, desc_l_ref, w2_ref, w3_ref,
    load_sem, send_sem, recv_sem,
):
    b = lax.axis_index("brick")
    s = lax.axis_index("slab")
    below = (lax.rem(b + NB - 1, NB), s)
    above = (lax.rem(b + 1, NB), s)
    barrier = pltpu.get_barrier_semaphore()
    for neighbour in (below, above):
        pl.semaphore_signal(barrier, inc=1, device_id=neighbour, device_id_type=MESH)

    sources = (
        table_any, first_any, second_any, third_any, neigh_any, pos_any, typ_any, count_any,
        e_in_any, w_in_any, e_hid_any, w_hid_any, e_out_any, w_out_any, base_any,
        cx_any, cy_any, cz_any, frac_any, z_any,
    )
    targets = (
        table_ref, first_ref, second_ref, third_ref, neigh_ref, pos_ref, typ_ref, count_ref,
        e_in_ref, w_in_ref, e_hid_ref, w_hid_ref, e_out_ref, w_out_ref, base_ref,
        cx_ref, cy_ref, cz_ref, frac_ref, z_ref,
    )
    loads = [
        pltpu.make_async_copy(source, target, load_sem.at[i])
        for i, (source, target) in enumerate(zip(sources, targets, strict=True))
    ]
    for load in loads:
        load.start()

    pl.semaphore_wait(barrier, 2)
    ghosts = []
    plan = (
        (above, pos_any, low_pos), (above, typ_any, low_typ), (above, snd_any, low_snd),
        (below, pos_any, upp_pos), (below, typ_any, upp_typ), (below, snd_any, upp_snd),
    )
    for i, (device, source, target) in enumerate(plan):
        ghosts.append(
            pltpu.make_async_remote_copy(
                src_ref=source,
                dst_ref=target,
                send_sem=send_sem.at[i],
                recv_sem=recv_sem.at[i],
                device_id=device,
                device_id_type=MESH,
            )
        )
    for ghost in ghosts:
        ghost.start()

    for load in loads[:4]:
        load.wait()
    f1 = lax.dot_general(table_ref[0:32, 0:25], first_ref[...], NT, precision=HIGHEST)
    oxygen, hydrogen = f1[:, 0:1], f1[:, 1:2]
    w2 = lax.dot_general(table_ref[32:96, 0:50], second_ref[...], NT, precision=HIGHEST)
    w2 = lax.dot_general(w2, table_ref[208:233, 0:96], NN, precision=HIGHEST)
    high, low = halves(w2)
    slot = lanes_iota((64, 96)) // 32
    w2_ref[...] = jnp.where(slot == 1, low.astype(F32), high.astype(F32)).astype(BF16)
    w3 = lax.dot_general(table_ref[96:208, 0:100], third_ref[...], NT, precision=HIGHEST)
    w3 = lax.dot_general(w3, table_ref[240:290, 0:192], NN, precision=HIGHEST)
    high, low = halves(w3)
    slot = lanes_iota((112, 192)) // 64
    w3_ref[...] = jnp.where(slot == 1, low.astype(F32), high.astype(F32)).astype(BF16)

    for load in loads[4:10]:
        load.wait()
    high, low = halves(e_in_ref[...])
    in_h_ref[0:240, :] = high
    in_l_ref[0:240, :] = low
    high, low = halves(w_in_ref[...])
    in_h_ref[240:480, :] = high
    in_l_ref[240:480, :] = low

    n = jnp.concatenate(
        [
            neigh_ref[0, :, 0:128],
            jnp.concatenate([neigh_ref[0, 0:32, 128:192], neigh_ref[0, 32:64, 128:192]], axis=1),
        ],
        axis=0,
    )

    def near(row):
        return row[:, 0:128]

    def far(row):
        return jnp.concatenate([row[:, 128:192], row[:, 128:192]], axis=1)

    def by_atom(row):
        return jnp.concatenate(
            [jnp.broadcast_to(near(row), (64, 128)), jnp.broadcast_to(far(row), (32, 128))], axis=0
        )

    own_index = (n - 96) & 127
    lower_index = n & 127
    upper_index = (n - 288) & 127
    row96 = rows_iota((96, 128))
    slot = jnp.where(row96 < 64, row96, row96 - 64 + jnp.where(lanes_iota((96, 128)) < 64, 0, 32))
    live = slot < by_atom(count_ref[...])

    for ghost in ghosts:
        ghost.wait_recv()

    low_snd_row = low_snd[...]
    upp_snd_row = upp_snd[...]
    low_list = jnp.concatenate([low_snd_row[:, 96:192], low_snd_row[:, 0:32]], axis=1)
    upp_list = upp_snd_row[:, 0:128]

    def ghost_row(row, index):
        index = jnp.broadcast_to(index, (8, 128))
        value = jnp.where(index < 128, pick(near(row), index & 127), pick(far(row), index & 127))
        return value[0:1]

    gathered = []
    for c in range(4):
        own = pos_ref[c] if c < 3 else typ_ref[...].astype(F32)
        low = low_pos[c] if c < 3 else low_typ[...].astype(F32)
        upp = upp_pos[c] if c < 3 else upp_typ[...].astype(F32)
        value = jnp.where(n < 224, pick(near(own), own_index), pick(far(own), own_index))
        value = jnp.where(n < 96, pick(ghost_row(low, low_list), lower_index), value)
        value = jnp.where(n >= 288, pick(ghost_row(upp, upp_list), upper_index), value)
        if c < 3:
            value = value - by_atom(own)
        gathered.append(value)
    squared = gathered[0] * gathered[0] + gathered[1] * gathered[1] + gathered[2] * gathered[2]
    smooth = jnp.where(live, 1.0 / (1.0 + squared), 0.0)
    env_ref[0] = smooth
    for c in range(3):
        env_ref[c + 1] = smooth * gathered[c]
    env_ref[4] = gathered[3]
    moment_ref[...] = jnp.zeros_like(moment_ref)

    oxygen_wide = jnp.broadcast_to(oxygen, (32, 128))
    hydrogen_wide = jnp.broadcast_to(hydrogen, (32, 128))

    def chunk(step, carry):
        at = pl.multiple_of(step * 8, 8)
        tile = step // 8
        first = []
        for r in range(8):
            sm = env_ref[0, pl.ds(at + r, 1), :]
            kind = env_ref[4, pl.ds(at + r, 1), :]
            mixing = jnp.where(kind > 0.5, hydrogen_wide, oxygen_wide)
            first.append(jnp.tanh(sm * mixing))
        first = jnp.concatenate(first, axis=1)
        high, low = halves(first)
        second = dot(w2_ref[...], jnp.concatenate([high, high, low], axis=0))
        second = jnp.tanh(second[:56]) + jnp.concatenate([first[:24], first], axis=0)
        padded = jnp.concatenate([second, jnp.zeros((8, 1024), F32)], axis=0)
        high, low = halves(padded)
        third = dot(w3_ref[...], jnp.concatenate([high, high, low], axis=0))
        third = jnp.tanh(third[:104]) + jnp.concatenate([second[:48], second], axis=0)
        for c in range(4):
            total = None
            for r in range(8):
                part = third[:, r * 128 : (r + 1) * 128] * env_ref[c, pl.ds(at + r, 1), :]
                total = part if total is None else total + part
            moment_ref[tile, c] += total
        return carry

    lax.fori_loop(0, 12, chunk, 0)

    for c in range(4):
        moment_ref[0, c] = moment_ref[0, c] * (1.0 / 64.0)
        value = moment_ref[1, c]
        moment_ref[1, c] = (value + pltpu.roll(value, 64, 1)) * (1.0 / 64.0)
    for tile in range(2):
        factors = [moment_ref[tile, c, 0:16, :] for c in range(4)]
        for m, place in enumerate(places()):
            value = None
            for c in range(4):
                term = moment_ref[tile, c, place : place + 1, :] * factors[c]
                value = term if value is None else value + term
            high, low = halves(value)
            desc_h_ref[m * 16 : m * 16 + 16, tile * 128 : (tile + 1) * 128] = high
            desc_l_ref[m * 16 : m * 16 + 16, tile * 128 : (tile + 1) * 128] = low

    both = jnp.tanh(dot3((in_h_ref[...], in_l_ref[...]), (desc_h_ref[...], desc_l_ref[...])))
    for load in loads[10:]:
        load.wait()

    def network(hidden, hid_ref, out_ref):
        for layer in range(2):
            hidden = jnp.tanh(dot3(halves(hidden), halves(hid_ref[layer]))) + hidden
        row = jnp.broadcast_to(out_ref[...], (16, 240))
        return dot3(halves(row), halves(hidden), NT)[0:1, 0:A]

    energy = network(both[:240].T, e_hid_ref, e_out_ref)
    shift = network(both[240:].T, w_hid_ref, w_out_ref)
    charge = jnp.where(typ_ref[...] == 1, base_ref[0:1, 1:2], base_ref[0:1, 0:1]) + shift
    scal_ref[...] = jnp.concatenate([energy, charge, jnp.zeros((6, A), F32)], axis=0)

    wxy, wz = spreads(cx_ref, cy_ref, cz_ref, frac_ref)
    grid = dot3(halves(wxy), halves(wz * charge), NT)
    spectrum = dot3(halves(grid), (z_ref[0:256, :], z_ref[256:512, :]))
    chunk_lane = lanes_iota((WY, 128)) // 16
    for s_to in range(NS):
        tile, chunk_from = divmod(s_to, 8)
        for half in range(2):
            out = jnp.zeros((WY, 128), F32)
            for x in range(8 * half, min(8 * half + 8, WX)):
                source = spectrum[x * WY : (x + 1) * WY, tile * 128 : (tile + 1) * 128]
                shift_by = 16 * (x % 8 - chunk_from) % 128
                if shift_by:
                    source = pltpu.roll(source, shift_by, 1)
                out = jnp.where(chunk_lane == x % 8, source, out)
            send_ref[s_to, :, half * 128 : (half + 1) * 128] = out
    for ghost in ghosts:
        ghost.wait_send()


def solve_kernel(
    send_ref, yh_ref, yl_ref, lh_ref, ll_ref, rh_ref, rl_ref, tc_ref, ts_ref,
    rbh_ref, rbl_ref, lbh_ref, lbl_ref, ybh_ref, ybl_ref,
    out_ref,
    in1, out2, in2, out3, in3, out4,
    send1, recv1, send2, recv2, send3, recv3, send4, recv4,
):
    b = lax.axis_index("brick")
    s = lax.axis_index("slab")

    barrier = pltpu.get_barrier_semaphore()

    def greet_slab(i, carry):
        pl.semaphore_signal(barrier, inc=1, device_id=(b, lax.rem(s + i, NS)), device_id_type=MESH)
        return carry

    def greet_brick(i, carry):
        pl.semaphore_signal(barrier, inc=1, device_id=(lax.rem(b + i, NB), s), device_id_type=MESH)
        return carry

    lax.fori_loop(1, NS, greet_slab, 0)
    lax.fori_loop(1, NB, greet_brick, 0)
    pl.semaphore_wait(barrier, NS + NB - 2)

    def over_slab(source, target, send_sem, recv_sem):
        def copy(i):
            to = lax.rem(s + i, NS)
            return pltpu.make_async_remote_copy(
                src_ref=source.at[to],
                dst_ref=target.at[s],
                send_sem=send_sem.at[to],
                recv_sem=recv_sem.at[s],
                device_id=(b, to),
                device_id_type=MESH,
            )

        def arrival(i):
            frm = lax.rem(s + i, NS)
            return pltpu.make_async_remote_copy(
                src_ref=source.at[frm],
                dst_ref=target.at[frm],
                send_sem=send_sem.at[frm],
                recv_sem=recv_sem.at[frm],
                device_id=(b, frm),
                device_id_type=MESH,
            )

        def start(i, carry):
            copy(i).start()
            return carry

        def wait(i, carry):
            arrival(i).wait_recv()
            return carry

        def drain(i, carry):
            copy(i).wait_send()
            return carry

        lax.fori_loop(1, NS, start, 0)
        target[s] = source[s]
        lax.fori_loop(1, NS, wait, 0)
        return lambda: lax.fori_loop(1, NS, drain, 0)

    def over_brick(source, target, send_sem, recv_sem):
        def copy(i):
            to = lax.rem(b + i, NB)
            return pltpu.make_async_remote_copy(
                src_ref=source.at[to],
                dst_ref=target.at[b],
                send_sem=send_sem.at[to],
                recv_sem=recv_sem.at[b],
                device_id=(to, s),
                device_id_type=MESH,
            )

        def arrival(i):
            frm = lax.rem(b + i, NB)
            return pltpu.make_async_remote_copy(
                src_ref=source.at[frm],
                dst_ref=target.at[frm],
                send_sem=send_sem.at[frm],
                recv_sem=recv_sem.at[frm],
                device_id=(frm, s),
                device_id_type=MESH,
            )

        def start(i, carry):
            copy(i).start()
            return carry

        def wait(i, carry):
            arrival(i).wait_recv()
            return carry

        def drain(i, carry):
            copy(i).wait_send()
            return carry

        lax.fori_loop(1, NB, start, 0)
        target[b] = source[b]
        lax.fori_loop(1, NB, wait, 0)
        return lambda: lax.fori_loop(1, NB, drain, 0)

    drain1 = over_slab(send_ref, in1, send1, recv1)
    data = halves(in1[...].reshape(NS * WY, NG))
    out2[...] = dot3((yh_ref[...], yl_ref[...]), data).reshape(NB, 8, NG)
    drain2 = over_brick(out2, in2, send2, recv2)

    row = rows_iota((256, 128))
    lane = lanes_iota((256, 128))

    def kappa(index):
        folded = jnp.minimum(index, NG - index)
        return folded.astype(F32) * (2.0 * math.pi / NG)

    kx = kappa(row // 8 + 32 * (lane // 16))
    ky = kappa(b * 8 + row % 8)
    kz = kappa(s * 16 + lane % 16)
    squared = kx * kx + ky * ky + kz * kz
    root = jnp.where(squared == 0.0, 1.0, 0.0)
    green = (1.0 - root) * jnp.exp(-0.5 * squared) / (squared + root) * (1.0 / NG)
    green = jnp.concatenate([green, green], axis=1)

    data = halves(in2[...].reshape(256, NG))
    both = dot3((lh_ref[...], ll_ref[...]), data)
    uc, us = both[:256], both[256:]
    tc, ts = tc_ref[...], ts_ref[...]
    turned = jnp.concatenate([uc * tc - us * ts, -(uc * ts + us * tc)], axis=1)
    modes = dot3(halves(turned), (rh_ref[...], rl_ref[...])) * green
    back = dot3(halves(modes), (rbh_ref[...], rbl_ref[...]))
    vr, vi = back[:, :256], back[:, 256:]
    turned = jnp.concatenate([vr * tc - vi * ts, vr * ts + vi * tc], axis=0)
    out3[...] = dot3((lbh_ref[...], lbl_ref[...]), halves(turned)).reshape(NB, 8, NG)
    drain3 = over_brick(out3, in3, send3, recv3)
    data = halves(in3[...].reshape(256, NG))
    out4[...] = dot3((ybh_ref[...], ybl_ref[...]), data).reshape(NS, WY, NG)
    drain4 = over_slab(out4, out_ref, send4, recv4)
    drain1()
    drain2()
    drain3()
    drain4()


def sample_kernel(
    in_ref, cx_ref, cy_ref, cz_ref, frac_ref, scal_ref, zh_ref, zl_ref, energy_ref, pot_ref, modes_ref
):
    chunk_lane = lanes_iota((WY, 128)) // 16
    for x in range(WX):
        half, chunk_from = divmod(x, 8)
        for tile in range(2):
            out = jnp.zeros((WY, 128), F32)
            for c in range(8):
                source = in_ref[8 * tile + c, :, half * 128 : (half + 1) * 128]
                shift_by = 16 * (c - chunk_from) % 128
                if shift_by:
                    source = pltpu.roll(source, shift_by, 1)
                out = jnp.where(chunk_lane == c, source, out)
            modes_ref[x * WY : (x + 1) * WY, tile * 128 : (tile + 1) * 128] = out
    potential = dot3(halves(modes_ref[...]), (zh_ref[...], zl_ref[...]))
    for x in range(CX):
        pot_ref[x] = potential[x * WY : x * WY + CY]
    wxy, wz = spreads(cx_ref, cy_ref, cz_ref, frac_ref)
    sampled = dot3(halves(potential), halves(wz))
    at = jnp.sum(sampled * wxy, axis=0, keepdims=True)
    energy_ref[...] = scal_ref[0:1, :] + 0.5 * scal_ref[1:2, :] * at


VMEM = pl.BlockSpec(memory_space=pltpu.VMEM)
HBM = pl.BlockSpec(memory_space=pltpu.HBM)


def per_device(
    positions, types, neighbours, neighbour_count, send_index, cell_x, cell_y, cell_z, spline_fraction,
    embed_first, embed_second, embed_third, energy_in, energy_hidden, energy_out,
    wannier_in, wannier_hidden, wannier_out, charge_base,
):
    tables = transform_tables()
    scalars, send = pl.pallas_call(
        atoms_kernel,
        out_shape=(
            jax.ShapeDtypeStruct((8, A), F32),
            jax.ShapeDtypeStruct((NS, WY, NG), F32),
        ),
        in_specs=[HBM] * 21,
        out_specs=(VMEM, VMEM),
        scratch_shapes=[
            pltpu.VMEM((3, 1, A), F32),
            pltpu.VMEM((1, A), jnp.int32),
            pltpu.VMEM((1, 64, A), jnp.int32),
            pltpu.VMEM((1, A), jnp.int32),
            pltpu.VMEM((1, A), jnp.int32),
            pltpu.VMEM((1, A), jnp.int32),
            pltpu.VMEM((1, A), jnp.int32),
            pltpu.VMEM((3, 1, A), F32),
            pltpu.VMEM((2, 25), F32),
            pltpu.VMEM((25, 50), F32),
            pltpu.VMEM((50, 100), F32),
            pltpu.VMEM((240, 1600), F32),
            pltpu.VMEM((2, 240, 240), F32),
            pltpu.VMEM((1, 240), F32),
            pltpu.VMEM((240, 1600), F32),
            pltpu.VMEM((2, 240, 240), F32),
            pltpu.VMEM((1, 240), F32),
            pltpu.VMEM((1, 2), F32),
            pltpu.VMEM((296, 256), F32),
            pltpu.VMEM((512, 256), BF16),
            pltpu.VMEM((3, 1, A), F32),
            pltpu.VMEM((1, A), jnp.int32),
            pltpu.VMEM((1, A), jnp.int32),
            pltpu.VMEM((3, 1, A), F32),
            pltpu.VMEM((1, A), jnp.int32),
            pltpu.VMEM((1, A), jnp.int32),
            pltpu.VMEM((5, 96, 128), F32),
            pltpu.VMEM((2, 4, 104, 128), F32),
            pltpu.VMEM((480, 1600), BF16),
            pltpu.VMEM((480, 1600), BF16),
            pltpu.VMEM((1600, 256), BF16),
            pltpu.VMEM((1600, 256), BF16),
            pltpu.VMEM((64, 96), BF16),
            pltpu.VMEM((112, 192), BF16),
            pltpu.SemaphoreType.DMA((LOADED,)),
            pltpu.SemaphoreType.DMA((6,)),
            pltpu.SemaphoreType.DMA((6,)),
        ],
        compiler_params=pltpu.CompilerParams(
            collective_id=2, has_side_effects=True, vmem_limit_bytes=60 * MIB
        ),
        name="atoms",
    )(
        positions, types, send_index, jnp.swapaxes(neighbours, 1, 2), neighbour_count,
        cell_x, cell_y, cell_z, spline_fraction,
        embed_first, embed_second, embed_third,
        energy_in.T, energy_hidden, energy_out.reshape(1, -1),
        wannier_in.T, wannier_hidden, wannier_out.reshape(1, -1), charge_base.reshape(1, 2),
        embedding_tables(), np.concatenate(tables["z"]),
    )

    received = pl.pallas_call(
        solve_kernel,
        out_shape=jax.ShapeDtypeStruct((NS, WY, NG), F32),
        in_specs=[VMEM] * 15,
        out_specs=VMEM,
        scratch_shapes=[
            pltpu.VMEM((NS, WY, NG), F32),
            pltpu.VMEM((NB, 8, NG), F32),
            pltpu.VMEM((NB, 8, NG), F32),
            pltpu.VMEM((NB, 8, NG), F32),
            pltpu.VMEM((NB, 8, NG), F32),
            pltpu.VMEM((NS, WY, NG), F32),
            pltpu.SemaphoreType.DMA((NS,)),
            pltpu.SemaphoreType.DMA((NS,)),
            pltpu.SemaphoreType.DMA((NB,)),
            pltpu.SemaphoreType.DMA((NB,)),
            pltpu.SemaphoreType.DMA((NB,)),
            pltpu.SemaphoreType.DMA((NB,)),
            pltpu.SemaphoreType.DMA((NS,)),
            pltpu.SemaphoreType.DMA((NS,)),
        ],
        compiler_params=pltpu.CompilerParams(
            collective_id=1, has_side_effects=True, vmem_limit_bytes=40 * MIB
        ),
        name="solve",
    )(
        send, *tables["y"], *tables["left"], *tables["right"], *tables["twist"],
        *tables["right_back"], *tables["left_back"], *tables["y_back"],
    )

    energy, potential = pl.pallas_call(
        sample_kernel,
        out_shape=(
            jax.ShapeDtypeStruct((1, A), F32),
            jax.ShapeDtypeStruct((CX, CY, NG), F32),
        ),
        in_specs=[VMEM] * 8,
        out_specs=(VMEM, VMEM),
        scratch_shapes=[pltpu.VMEM((WX * WY, NG), F32)],
        compiler_params=pltpu.CompilerParams(vmem_limit_bytes=40 * MIB),
        name="sample",
    )(received, cell_x, cell_y, cell_z, spline_fraction, scalars, *tables["z_back"])
    return energy, potential


def solution(mesh):
    row = P("slab", "brick")
    three = P(None, "slab", "brick")
    placed = (three, row, P("slab", "brick", None), row, row, row, row, row, three) + (P(),) * 10
    return jax.shard_map(
        per_device,
        mesh=mesh,
        in_specs=placed,
        out_specs=(row, P("brick", "slab", None)),
        check_vma=False,
    )
```

```python
import math

import jax
import jax.numpy as jnp
import numpy as np
from jax import lax
from jax.experimental import pallas as pl
from jax.experimental.pallas import tpu as pltpu
from jax.sharding import PartitionSpec as P

NG = 256
A = 192
NB = 32
NS = 16
CX = 8
CY = 16
MIB = 1024 * 1024
F32 = jnp.float32
BF16 = jnp.bfloat16
HIGHEST = lax.Precision.HIGHEST
MESH = pl.DeviceIdType.MESH

NN = (((1,), (0,)), ((), ()))
NT = (((1,), (1,)), ((), ()))


def split(table):
    table = np.asarray(table, np.float64)
    high = np.asarray(table, np.float32).astype(jnp.bfloat16)
    low = (table - high.astype(np.float64)).astype(np.float32).astype(jnp.bfloat16)
    return high, low


def real_basis():
    n = np.arange(NG)[:, None]
    j = np.arange(NG)[None, :]
    phase = 2.0 * np.pi * ((n * j) % NG) / NG
    basis = np.where(j <= NG // 2, np.cos(phase), np.sin(phase)) * math.sqrt(2.0 / NG)
    basis[:, 0] = 1.0 / 16.0
    basis[:, NG // 2] = np.where(np.arange(NG) % 2 == 0, 1.0, -1.0) / 16.0
    return basis


def transform_tables():
    basis = real_basis()
    b = np.arange(NB)
    angle = 2.0 * np.pi * np.outer(b, b) / NB
    eye8 = np.eye(8)
    left = np.concatenate([np.kron(np.cos(angle), eye8), np.kron(np.sin(angle), eye8)], axis=0)
    xi = np.arange(8)
    small = 2.0 * np.pi * np.outer(xi, xi) / 8
    eye16 = np.eye(16)
    cos_m = np.kron(np.cos(small), eye16)
    sin_m = np.kron(np.sin(small), eye16)
    right = np.block([[cos_m, -sin_m], [sin_m, cos_m]])
    high, low = zip(*(split(table) for table in (basis, basis.T, left, right)), strict=True)
    twist = 2.0 * np.pi * np.repeat(b, 8)[:, None] * np.repeat(xi, 16)[None, :] / NG
    twist = np.concatenate([np.cos(twist), np.sin(twist)]).astype(np.float32)
    return np.concatenate(high), np.concatenate(low), twist


def second_rows():
    rows = list(range(24)) + list(range(25, 49)) + [24, 49, 24, 49]
    return rows


def third_rows():
    second = second_rows()
    return [f for f in second[:48]] + [50 + f for f in second[:48]] + [24, 49, 74, 99]


def one_hot(rows, height, width):
    table = np.zeros((height, width), np.float32)
    for row, feature in enumerate(rows):
        table[row, feature] = 1.0
    return table


def embedding_tables():
    first = one_hot(list(range(25)) + [24, 24, 24], 32, 25)
    second = one_hot(second_rows(), 64, 50)
    third = one_hot(third_rows(), 112, 100)
    columns_first = np.tile(np.eye(25, 32, dtype=np.float32), (1, 3))
    placed = np.zeros((50, 64), np.float32)
    for row, feature in enumerate(second_rows()[:50]):
        placed[feature, row] = 1.0
    columns_second = np.tile(placed, (1, 3))
    table = np.zeros((296, 256), np.float32)
    table[0:32, :25] = first
    table[32:96, :50] = second
    table[96:208, :100] = third
    table[208:233, :96] = columns_first
    table[240:290, :192] = columns_second
    return table


def places():
    rows = third_rows()
    return [rows.index(feature) for feature in range(100)]


def halves(values):
    high = values.astype(BF16)
    low = (values - high.astype(F32)).astype(BF16)
    return high, low


def dot(a, b, dims=NN):
    return lax.dot_general(a, b, dims, preferred_element_type=F32)


def dot3(a, b, dims=NN):
    return dot(a[0], b[0], dims) + (dot(a[0], b[1], dims) + dot(a[1], b[0], dims))


def dot3_narrow(a, b):
    both = dot(a[0], jnp.concatenate([b[0], b[1]], axis=1))
    return both[:, :128] + (both[:, 128:] + dot(a[1], b[0]))


def lanes_iota(shape):
    return lax.broadcasted_iota(jnp.int32, shape, 1)


def rows_iota(shape):
    return lax.broadcasted_iota(jnp.int32, shape, 0)


def pick(row, index):
    table = jnp.broadcast_to(row, index.shape)
    return jnp.take_along_axis(table, index, axis=1, mode="promise_in_bounds")


def spline_rows(u):
    cubed = u * u * u
    square = u * u
    rest = 1.0 - u
    return (
        rest * rest * rest / 6.0,
        (3.0 * cubed - 6.0 * square + 4.0) / 6.0,
        (-3.0 * cubed + 3.0 * square + 3.0 * u + 1.0) / 6.0,
        cubed / 6.0,
    )


def place_rows(start, weights, height, wrap):
    offset = rows_iota((height, A)) - start
    if wrap:
        offset = offset & (wrap - 1)
    result = jnp.zeros((height, A), F32)
    for step in range(4):
        result = jnp.where(offset == step, weights[step], result)
    return result


LOADED = 22


def kernel(
    pos_any, typ_any, snd_any, neigh_any, count_any, cx_any, cy_any, cz_any, frac_any,
    first_any, second_any, third_any, e_in_any, e_hid_any, e_out_any, w_in_any, w_hid_any, w_out_any,
    base_any, table_any, high_any, low_any, twist_any,
    energy_ref, pot_any,
    pos_ref, typ_ref, neigh_ref, count_ref, cx_ref, cy_ref, cz_ref, frac_ref,
    first_ref, second_ref, third_ref, e_in_ref, e_hid_ref, e_out_ref, w_in_ref, w_hid_ref, w_out_ref,
    base_ref, table_ref, high_ref, low_ref, twist_ref,
    low_pos, low_typ, low_snd, upp_pos, upp_typ, upp_snd,
    env_ref, moment_ref, in_h_ref, in_l_ref, desc_h_ref, desc_l_ref, w2_ref, w3_ref,
    charge_ref, charges_ref, wxy_ref, wz_h_ref, wz_l_ref, green_ref,
    out1, in1, out2, in2, out3, in3, out4, in4, modes_ref, pot_ref, part_ref, back_ref,
    load_sem, pot_sem, ghost_send, ghost_recv, cell_send, cell_recv, charge_send, charge_recv,
    part_send, part_recv, send1, recv1, send2, recv2, send3, recv3, send4, recv4,
):
    b = lax.axis_index("brick")
    s = lax.axis_index("slab")
    b_up, b_down = lax.rem(b + 1, NB), lax.rem(b + NB - 1, NB)
    s_up, s_down = lax.rem(s + 1, NS), lax.rem(s + NS - 1, NS)
    below, above = (b_down, s), (b_up, s)
    shifts = ((0, 0), (1, 0), (0, 1), (1, 1))
    onward = ((b, s), (b_up, s), (b, s_up), (b_up, s_up))
    origin = ((b, s), (b_down, s), (b, s_down), (b_down, s_down))

    barrier = pltpu.get_barrier_semaphore()

    def greet_slab(i, carry):
        pl.semaphore_signal(barrier, inc=1, device_id=(b, lax.rem(s + i, NS)), device_id_type=MESH)
        return carry

    def greet_brick(i, carry):
        pl.semaphore_signal(barrier, inc=1, device_id=(lax.rem(b + i, NB), s), device_id_type=MESH)
        return carry

    lax.fori_loop(1, NS, greet_slab, 0)
    lax.fori_loop(1, NB, greet_brick, 0)
    for device in (onward[3], origin[3]):
        pl.semaphore_signal(barrier, inc=1, device_id=device, device_id_type=MESH)

    sources = (
        table_any, first_any, second_any, third_any, e_in_any, w_in_any,
        neigh_any, pos_any, typ_any, count_any,
        e_hid_any, w_hid_any, e_out_any, w_out_any, base_any,
        cx_any, cy_any, cz_any, frac_any, high_any, low_any, twist_any,
    )
    targets = (
        table_ref, first_ref, second_ref, third_ref, e_in_ref, w_in_ref,
        neigh_ref, pos_ref, typ_ref, count_ref,
        e_hid_ref, w_hid_ref, e_out_ref, w_out_ref, base_ref,
        cx_ref.at[0], cy_ref.at[0], cz_ref.at[0], frac_ref.at[0], high_ref, low_ref, twist_ref,
    )
    loads = [
        pltpu.make_async_copy(source, target, load_sem.at[i])
        for i, (source, target) in enumerate(zip(sources, targets, strict=True))
    ]
    for load in loads:
        load.start()

    pl.semaphore_wait(barrier, NS + NB)

    def remote(source, target, send_sem, recv_sem, device):
        return pltpu.make_async_remote_copy(
            src_ref=source, dst_ref=target, send_sem=send_sem, recv_sem=recv_sem,
            device_id=device, device_id_type=MESH,
        )

    plan = (
        (above, pos_any, low_pos), (above, typ_any, low_typ), (above, snd_any, low_snd),
        (below, pos_any, upp_pos), (below, typ_any, upp_typ), (below, snd_any, upp_snd),
    )
    ghosts = [
        remote(source, target, ghost_send.at[i], ghost_recv.at[i], device)
        for i, (device, source, target) in enumerate(plan)
    ]
    for ghost in ghosts:
        ghost.start()
    cells = []
    for n in range(1, 4):
        pairs = ((cx_any, cx_ref), (cy_any, cy_ref), (cz_any, cz_ref), (frac_any, frac_ref))
        for i, (source, target) in enumerate(pairs):
            k = (n - 1) * 4 + i
            cells.append(
                remote(source, target.at[n], cell_send.at[k], cell_recv.at[k], onward[n])
            )
    for cell in cells:
        cell.start()

    row = rows_iota((256, 128))
    lane = lanes_iota((256, 128))

    def kappa(index):
        folded = jnp.minimum(index, NG - index)
        return folded.astype(F32) * (2.0 * math.pi / NG)

    kx = kappa(row // 8 + 32 * (lane // 16))
    ky = kappa(b * 8 + row % 8)
    kz = kappa(s * 16 + lane % 16)
    squared = kx * kx + ky * ky + kz * kz
    root = jnp.where(squared == 0.0, 1.0, 0.0)
    green_ref[...] = (1.0 - root) * jnp.exp(-0.5 * squared) / (squared + root) * (1.0 / NG)

    for load in loads[:4]:
        load.wait()
    f1 = lax.dot_general(table_ref[0:32, 0:25], first_ref[...], NT, precision=HIGHEST)
    oxygen, hydrogen = f1[:, 0:1], f1[:, 1:2]
    w2 = lax.dot_general(table_ref[32:96, 0:50], second_ref[...], NT, precision=HIGHEST)
    w2 = lax.dot_general(w2, table_ref[208:233, 0:96], NN, precision=HIGHEST)
    high, low = halves(w2)
    slot = lanes_iota((64, 96)) // 32
    w2_ref[...] = jnp.where(slot == 1, low.astype(F32), high.astype(F32)).astype(BF16)
    w3 = lax.dot_general(table_ref[96:208, 0:100], third_ref[...], NT, precision=HIGHEST)
    w3 = lax.dot_general(w3, table_ref[240:290, 0:192], NN, precision=HIGHEST)
    high, low = halves(w3)
    slot = lanes_iota((112, 192)) // 64
    w3_ref[...] = jnp.where(slot == 1, low.astype(F32), high.astype(F32)).astype(BF16)

    for load in loads[4:10]:
        load.wait()
    high, low = halves(e_in_ref[...])
    in_h_ref[0:240, :] = high
    in_l_ref[0:240, :] = low
    high, low = halves(w_in_ref[...])
    in_h_ref[240:480, :] = high
    in_l_ref[240:480, :] = low

    n = jnp.concatenate(
        [
            neigh_ref[0, :, 0:128],
            jnp.concatenate([neigh_ref[0, 0:32, 128:192], neigh_ref[0, 32:64, 128:192]], axis=1),
        ],
        axis=0,
    )

    def near(row):
        return row[:, 0:128]

    def far(row):
        return jnp.concatenate([row[:, 128:192], row[:, 128:192]], axis=1)

    def by_atom(row):
        return jnp.concatenate(
            [jnp.broadcast_to(near(row), (64, 128)), jnp.broadcast_to(far(row), (32, 128))], axis=0
        )

    own_index = (n - 96) & 127
    lower_index = n & 127
    upper_index = (n - 288) & 127
    row96 = rows_iota((96, 128))
    slot = jnp.where(row96 < 64, row96, row96 - 64 + jnp.where(lanes_iota((96, 128)) < 64, 0, 32))
    live = slot < by_atom(count_ref[...])

    for ghost in ghosts:
        ghost.wait_recv()

    low_snd_row = low_snd[...]
    upp_snd_row = upp_snd[...]
    low_list = jnp.concatenate([low_snd_row[:, 96:192], low_snd_row[:, 0:32]], axis=1)
    upp_list = upp_snd_row[:, 0:128]

    def ghost_row(row, index):
        index = jnp.broadcast_to(index, (8, 128))
        value = jnp.where(index < 128, pick(near(row), index & 127), pick(far(row), index & 127))
        return value[0:1]

    gathered = []
    for c in range(4):
        own = pos_ref[c] if c < 3 else typ_ref[...].astype(F32)
        low = low_pos[c] if c < 3 else low_typ[...].astype(F32)
        upp = upp_pos[c] if c < 3 else upp_typ[...].astype(F32)
        value = jnp.where(n < 224, pick(near(own), own_index), pick(far(own), own_index))
        value = jnp.where(n < 96, pick(ghost_row(low, low_list), lower_index), value)
        value = jnp.where(n >= 288, pick(ghost_row(upp, upp_list), upper_index), value)
        if c < 3:
            value = value - by_atom(own)
        gathered.append(value)
    squared = gathered[0] * gathered[0] + gathered[1] * gathered[1] + gathered[2] * gathered[2]
    smooth = jnp.where(live, 1.0 / (1.0 + squared), 0.0)
    env_ref[0] = smooth
    for c in range(3):
        env_ref[c + 1] = smooth * gathered[c]
    env_ref[4] = gathered[3]
    moment_ref[...] = jnp.zeros_like(moment_ref)

    oxygen_wide = jnp.broadcast_to(oxygen, (32, 128))
    hydrogen_wide = jnp.broadcast_to(hydrogen, (32, 128))

    def chunk(step, carry):
        at = pl.multiple_of(step * 8, 8)
        tile = step // 8
        first = []
        for r in range(8):
            sm = env_ref[0, pl.ds(at + r, 1), :]
            kind = env_ref[4, pl.ds(at + r, 1), :]
            mixing = jnp.where(kind > 0.5, hydrogen_wide, oxygen_wide)
            first.append(jnp.tanh(sm * mixing))
        first = jnp.concatenate(first, axis=1)
        high, low = halves(first)
        second = dot(w2_ref[...], jnp.concatenate([high, high, low], axis=0))
        second = jnp.tanh(second[:56]) + jnp.concatenate([first[:24], first], axis=0)
        padded = jnp.concatenate([second, jnp.zeros((8, 1024), F32)], axis=0)
        high, low = halves(padded)
        third = dot(w3_ref[...], jnp.concatenate([high, high, low], axis=0))
        third = jnp.tanh(third[:104]) + jnp.concatenate([second[:48], second], axis=0)
        for c in range(4):
            total = None
            for r in range(8):
                part = third[:, r * 128 : (r + 1) * 128] * env_ref[c, pl.ds(at + r, 1), :]
                total = part if total is None else total + part
            moment_ref[tile, c] += total
        return carry

    lax.fori_loop(0, 12, chunk, 0)

    for c in range(4):
        moment_ref[0, c] = moment_ref[0, c] * (1.0 / 64.0)
        value = moment_ref[1, c]
        moment_ref[1, c] = (value + pltpu.roll(value, 64, 1)) * (1.0 / 64.0)
    for tile in range(2):
        factors = [moment_ref[tile, c, 0:16, :] for c in range(4)]
        for m, place in enumerate(places()):
            value = None
            for c in range(4):
                term = moment_ref[tile, c, place : place + 1, :] * factors[c]
                value = term if value is None else value + term
            high, low = halves(value)
            desc_h_ref[m * 16 : m * 16 + 16, tile * 128 : (tile + 1) * 128] = high
            desc_l_ref[m * 16 : m * 16 + 16, tile * 128 : (tile + 1) * 128] = low

    both = jnp.tanh(dot3((in_h_ref[...], in_l_ref[...]), (desc_h_ref[...], desc_l_ref[...])))
    for load in loads[10:]:
        load.wait()

    def network(hidden, hid_ref, out_ref):
        for layer in range(2):
            hidden = jnp.tanh(dot3(halves(hidden), halves(hid_ref[layer]))) + hidden
        row = jnp.broadcast_to(out_ref[...], (16, 240))
        return dot3(halves(row), halves(hidden), NT)[0:1, 0:A]

    energy = network(both[:240].T, e_hid_ref, e_out_ref)
    shift = network(both[240:].T, w_hid_ref, w_out_ref)
    charge = jnp.where(typ_ref[...] == 1, base_ref[0:1, 1:2], base_ref[0:1, 0:1]) + shift
    charge_ref[...] = charge
    charges = [
        remote(charge_ref, charges_ref.at[n], charge_send.at[n], charge_recv.at[n], onward[n])
        for n in range(1, 4)
    ]
    for copy in charges:
        copy.start()

    for cell in cells:
        cell.wait_recv()
    grid = None
    for n, (dx, dy) in enumerate(shifts):
        wx = place_rows(cx_ref[n] - dx * CX, spline_rows(frac_ref[n, 0]), CX, 0)
        wy = place_rows(cy_ref[n] - dy * CY, spline_rows(frac_ref[n, 1]), CY, 0)
        high, low = halves(place_rows(cz_ref[n], spline_rows(frac_ref[n, 2]), NG, NG))
        wz_h_ref[n] = high
        wz_l_ref[n] = low
        wxy = jnp.concatenate([wx[x : x + 1] * wy for x in range(CX)], axis=0)
        wxy_ref[n] = wxy
    for n in range(4):
        if n:
            charges[n - 1].wait_recv()
        weighted = wxy_ref[n] * (charges_ref[n] if n else charge)
        part = dot3(halves(weighted), (wz_h_ref[n], wz_l_ref[n]), NT)
        grid = part if grid is None else grid + part

    def table(k, count=1):
        at = slice(k * NG, (k + count) * NG)
        return high_ref[at, :], low_ref[at, :]

    spectrum = dot3(halves(grid), table(0))
    chunk_lane = lanes_iota((CY, 128)) // 16
    for to in range(NS):
        tile, chunk_from = divmod(to, 8)
        out = jnp.zeros((CY, 128), F32)
        for x in range(CX):
            source = spectrum[x * CY : (x + 1) * CY, tile * 128 : (tile + 1) * 128]
            shift_by = 16 * (x - chunk_from) % 128
            if shift_by:
                source = pltpu.roll(source, shift_by, 1)
            out = jnp.where(chunk_lane == x, source, out)
        out1[to] = out

    def exchange(source, target, send_sem, recv_sem, me, count, device_of):
        def copy(i):
            to = lax.rem(me + i, count)
            return remote(
                source.at[to], target.at[me], send_sem.at[to], recv_sem.at[me], device_of(to)
            )

        def arrival(i):
            frm = lax.rem(me + count - i, count)
            return remote(
                source.at[frm], target.at[frm], send_sem.at[frm], recv_sem.at[frm], device_of(frm)
            )

        def start(i, carry):
            copy(i).start()
            return carry

        def wait(i, carry):
            arrival(i).wait_recv()
            return carry

        def drain(i, carry):
            copy(i).wait_send()
            return carry

        lax.fori_loop(1, count, start, 0)
        target[me] = source[me]
        lax.fori_loop(1, count, wait, 0)
        return lambda: lax.fori_loop(1, count, drain, 0)

    def over_slab(source, target, send_sem, recv_sem):
        return exchange(source, target, send_sem, recv_sem, s, NS, lambda to: (b, to))

    def over_brick(source, target, send_sem, recv_sem):
        return exchange(source, target, send_sem, recv_sem, b, NB, lambda to: (to, s))

    drains = [over_slab(out1, in1, send1, recv1)]
    data = halves(in1[...].reshape(NG, 128))
    out2[...] = dot3_narrow(table(1), data).reshape(NB, 8, 128)
    drains.append(over_brick(out2, in2, send2, recv2))

    data = halves(in2[...].reshape(NG, 128))
    both = dot3_narrow(table(2, 2), data)
    uc, us = both[:256], both[256:]
    tc, ts = twist_ref[0:256, :], twist_ref[256:512, :]
    turned = jnp.concatenate([uc * tc - us * ts, -(uc * ts + us * tc)], axis=1)
    green = green_ref[...]
    modes = dot3(halves(turned), table(4)) * jnp.concatenate([green, green], axis=1)
    back = dot3(halves(modes), table(4), NT)
    vr, vi = back[:, :128], back[:, 128:]
    real = dot3_narrow(table(2), halves(vr * tc - vi * ts))
    imag = dot3_narrow(table(3), halves(vr * ts + vi * tc))
    out3[...] = (real - imag).reshape(NB, 8, 128)
    drains.append(over_brick(out3, in3, send3, recv3))
    data = halves(in3[...].reshape(NG, 128))
    out4[...] = dot3_narrow(table(0), data).reshape(NS, CY, 128)
    drains.append(over_slab(out4, in4, send4, recv4))

    for x in range(CX):
        for tile in range(2):
            out = jnp.zeros((CY, 128), F32)
            for c in range(8):
                source = in4[8 * tile + c]
                shift_by = 16 * (c - x) % 128
                if shift_by:
                    source = pltpu.roll(source, shift_by, 1)
                out = jnp.where(chunk_lane == c, source, out)
            modes_ref[x * CY : (x + 1) * CY, tile * 128 : (tile + 1) * 128] = out
    potential = dot3(halves(modes_ref[...]), table(0), NT)
    pot_ref[...] = potential.reshape(CX, CY, NG)
    pot_copy = pltpu.make_async_copy(pot_ref, pot_any, pot_sem)
    pot_copy.start()

    data = halves(potential)
    returns = []
    for n in (1, 2, 3, 0):
        sampled = dot3(data, (wz_h_ref[n], wz_l_ref[n]))
        part_ref[n] = jnp.sum(sampled * wxy_ref[n], axis=0, keepdims=True)
        if n:
            copy = remote(part_ref.at[n], back_ref.at[n], part_send.at[n], part_recv.at[n], origin[n])
            copy.start()
            returns.append(copy)
    for drain in drains:
        drain()
    for copy in ghosts + cells + charges:
        copy.wait_send()
    for copy in returns:
        copy.wait_recv()
    at = part_ref[0] + back_ref[1] + back_ref[2] + back_ref[3]
    energy_ref[...] = energy + 0.5 * charge * at
    for copy in returns:
        copy.wait_send()
    pot_copy.wait()


def hand_over(energy_in, pot_in, energy_out, pot_out, energy_ref, pot_ref, sem):
    arriving = [
        pltpu.make_async_copy(energy_in, energy_ref, sem.at[0]),
        pltpu.make_async_copy(pot_in, pot_ref, sem.at[1]),
    ]
    leaving = [
        pltpu.make_async_copy(energy_ref, energy_out, sem.at[2]),
        pltpu.make_async_copy(pot_ref, pot_out, sem.at[3]),
    ]
    for copy in arriving:
        copy.start()
    for first, second in zip(arriving, leaving, strict=True):
        first.wait()
        second.start()
    for copy in leaving:
        copy.wait()


VMEM = pl.BlockSpec(memory_space=pltpu.VMEM)
ANY = pl.BlockSpec(memory_space=pl.ANY)
I32 = jnp.int32


def per_device(
    positions, types, neighbours, neighbour_count, send_index, cell_x, cell_y, cell_z, spline_fraction,
    embed_first, embed_second, embed_third, energy_in, energy_hidden, energy_out,
    wannier_in, wannier_hidden, wannier_out, charge_base,
):
    vmem = pltpu.VMEM
    dma = pltpu.SemaphoreType.DMA
    slab_block, brick_block = vmem((NS, CY, 128), F32), vmem((NB, 8, 128), F32)
    outs = (jax.ShapeDtypeStruct((1, A), F32), jax.ShapeDtypeStruct((CX, CY, NG), F32))
    results = tuple(
        pl.pallas_call(
            kernel,
            out_shape=outs,
            in_specs=[ANY] * 23,
            out_specs=(VMEM, ANY),
            scratch_shapes=[
                vmem((3, 1, A), F32), vmem((1, A), I32), vmem((1, 64, A), I32), vmem((1, A), I32),
                vmem((4, 1, A), I32), vmem((4, 1, A), I32), vmem((4, 1, A), I32), vmem((4, 3, 1, A), F32),
                vmem((2, 25), F32), vmem((25, 50), F32), vmem((50, 100), F32),
                vmem((240, 1600), F32), vmem((2, 240, 240), F32), vmem((1, 240), F32),
                vmem((240, 1600), F32), vmem((2, 240, 240), F32), vmem((1, 240), F32),
                vmem((1, 2), F32), vmem((296, 256), F32),
                vmem((5 * NG, NG), BF16), vmem((5 * NG, NG), BF16), vmem((2 * NG, 128), F32),
                vmem((3, 1, A), F32), vmem((1, A), I32), vmem((1, A), I32),
                vmem((3, 1, A), F32), vmem((1, A), I32), vmem((1, A), I32),
                vmem((5, 96, 128), F32), vmem((2, 4, 104, 128), F32),
                vmem((480, 1600), BF16), vmem((480, 1600), BF16),
                vmem((1600, 256), BF16), vmem((1600, 256), BF16),
                vmem((64, 96), BF16), vmem((112, 192), BF16),
                vmem((1, A), F32), vmem((4, 1, A), F32), vmem((4, 128, A), F32),
                vmem((4, NG, A), BF16), vmem((4, NG, A), BF16), vmem((NG, 128), F32),
                slab_block, slab_block, brick_block, brick_block,
                brick_block, brick_block, slab_block, slab_block,
                vmem((128, NG), F32), vmem((CX, CY, NG), F32), vmem((4, 1, A), F32), vmem((4, 1, A), F32),
                dma((LOADED,)), dma, dma((6,)), dma((6,)), dma((12,)), dma((12,)), dma((4,)), dma((4,)),
                dma((4,)), dma((4,)), dma((NS,)), dma((NS,)), dma((NB,)), dma((NB,)),
                dma((NB,)), dma((NB,)), dma((NS,)), dma((NS,)),
            ],
            compiler_params=pltpu.CompilerParams(
                collective_id=1, has_side_effects=True, vmem_limit_bytes=60 * MIB
            ),
            name="potential",
        )(
            positions, types, send_index, jnp.swapaxes(neighbours, 1, 2), neighbour_count,
            cell_x, cell_y, cell_z, spline_fraction,
            embed_first, embed_second, embed_third,
            energy_in.T, energy_hidden, energy_out.reshape(1, -1),
            wannier_in.T, wannier_hidden, wannier_out.reshape(1, -1), charge_base.reshape(1, 2),
            embedding_tables(), *transform_tables(),
        )
    )
    return pl.pallas_call(
        hand_over,
        out_shape=outs,
        in_specs=[ANY, ANY],
        out_specs=(ANY, ANY),
        scratch_shapes=[vmem((1, A), F32), vmem((CX, CY, NG), F32), dma((4,))],
        compiler_params=pltpu.CompilerParams(vmem_limit_bytes=60 * MIB),
        name="hand_over",
    )(*results)


def solution(mesh):
    row = P("slab", "brick")
    three = P(None, "slab", "brick")
    placed = (three, row, P("slab", "brick", None), row, row, row, row, row, three) + (P(),) * 10
    return jax.shard_map(
        per_device,
        mesh=mesh,
        in_specs=placed,
        out_specs=(row, P("brick", "slab", None)),
        check_vma=False,
    )
```

```python
import math

import jax
import jax.numpy as jnp
import numpy as np
from jax import lax
from jax.experimental import pallas as pl
from jax.experimental.pallas import tpu as pltpu
from jax.sharding import PartitionSpec as P

NG = 256
A = 192
NB = 32
NS = 16
CX = 8
CY = 16
MIB = 1024 * 1024
F32 = jnp.float32
BF16 = jnp.bfloat16
HIGHEST = lax.Precision.HIGHEST
MESH = pl.DeviceIdType.MESH

NN = (((1,), (0,)), ((), ()))
NT = (((1,), (1,)), ((), ()))


def split(table):
    table = np.asarray(table, np.float64)
    high = np.asarray(table, np.float32).astype(jnp.bfloat16)
    low = (table - high.astype(np.float64)).astype(np.float32).astype(jnp.bfloat16)
    return high, low


def real_basis():
    n = np.arange(NG)[:, None]
    j = np.arange(NG)[None, :]
    phase = 2.0 * np.pi * ((n * j) % NG) / NG
    basis = np.where(j <= NG // 2, np.cos(phase), np.sin(phase)) * math.sqrt(2.0 / NG)
    basis[:, 0] = 1.0 / 16.0
    basis[:, NG // 2] = np.where(np.arange(NG) % 2 == 0, 1.0, -1.0) / 16.0
    return basis


def transform_tables():
    basis = real_basis()
    b = np.arange(NB)
    angle = 2.0 * np.pi * np.outer(b, b) / NB
    eye8 = np.eye(8)
    left = np.concatenate([np.kron(np.cos(angle), eye8), np.kron(np.sin(angle), eye8)], axis=0)
    xi = np.arange(8)
    small = 2.0 * np.pi * np.outer(xi, xi) / 8
    eye16 = np.eye(16)
    cos_m = np.kron(np.cos(small), eye16)
    sin_m = np.kron(np.sin(small), eye16)
    right = np.block([[cos_m, -sin_m], [sin_m, cos_m]])
    high, low = zip(*(split(table) for table in (basis, basis.T, left, right)), strict=True)
    twist = 2.0 * np.pi * np.repeat(b, 8)[:, None] * np.repeat(xi, 16)[None, :] / NG
    twist = np.concatenate([np.cos(twist), np.sin(twist)]).astype(np.float32)
    return np.concatenate(high), np.concatenate(low), twist


def second_rows():
    rows = list(range(24)) + list(range(25, 49)) + [24, 49, 24, 49]
    return rows


def third_rows():
    second = second_rows()
    return [f for f in second[:48]] + [50 + f for f in second[:48]] + [24, 49, 74, 99]


def one_hot(rows, height, width):
    table = np.zeros((height, width), np.float32)
    for row, feature in enumerate(rows):
        table[row, feature] = 1.0
    return table


def embedding_tables():
    first = one_hot(list(range(25)) + [24, 24, 24], 32, 25)
    second = one_hot(second_rows(), 64, 50)
    third = one_hot(third_rows(), 112, 100)
    columns_first = np.tile(np.eye(25, 32, dtype=np.float32), (1, 3))
    placed = np.zeros((50, 64), np.float32)
    for row, feature in enumerate(second_rows()[:50]):
        placed[feature, row] = 1.0
    columns_second = np.tile(placed, (1, 3))
    table = np.zeros((296, 256), np.float32)
    table[0:32, :25] = first
    table[32:96, :50] = second
    table[96:208, :100] = third
    table[208:233, :96] = columns_first
    table[240:290, :192] = columns_second
    return table


def places():
    rows = third_rows()
    return [rows.index(feature) for feature in range(100)]


def halves(values):
    high = values.astype(BF16)
    low = (values - high.astype(F32)).astype(BF16)
    return high, low


def dot(a, b, dims=NN):
    return lax.dot_general(a, b, dims, preferred_element_type=F32)


def dot3(a, b, dims=NN):
    return dot(a[0], b[0], dims) + (dot(a[0], b[1], dims) + dot(a[1], b[0], dims))


def dot3_narrow(a, b):
    both = dot(a[0], jnp.concatenate([b[0], b[1]], axis=1))
    return both[:, :128] + (both[:, 128:] + dot(a[1], b[0]))


def lanes_iota(shape):
    return lax.broadcasted_iota(jnp.int32, shape, 1)


def rows_iota(shape):
    return lax.broadcasted_iota(jnp.int32, shape, 0)


def pick(row, index):
    table = jnp.broadcast_to(row, index.shape)
    return jnp.take_along_axis(table, index, axis=1, mode="promise_in_bounds")


def spline_rows(u):
    cubed = u * u * u
    square = u * u
    rest = 1.0 - u
    return (
        rest * rest * rest / 6.0,
        (3.0 * cubed - 6.0 * square + 4.0) / 6.0,
        (-3.0 * cubed + 3.0 * square + 3.0 * u + 1.0) / 6.0,
        cubed / 6.0,
    )


def place_rows(start, weights, height, wrap):
    offset = rows_iota((height, A)) - start
    if wrap:
        offset = offset & (wrap - 1)
    result = jnp.zeros((height, A), F32)
    for step in range(4):
        result = jnp.where(offset == step, weights[step], result)
    return result


LOADED = 22


def kernel(
    pos_any, typ_any, snd_any, neigh_any, count_any, cx_any, cy_any, cz_any, frac_any,
    first_any, second_any, third_any, e_in_any, e_hid_any, e_out_any, w_in_any, w_hid_any, w_out_any,
    base_any, table_any, high_any, low_any, twist_any,
    energy_ref, pot_any,
    pos_ref, typ_ref, neigh_ref, count_ref, cx_ref, cy_ref, cz_ref, frac_ref,
    first_ref, second_ref, third_ref, e_in_ref, e_hid_ref, e_out_ref, w_in_ref, w_hid_ref, w_out_ref,
    base_ref, table_ref, high_ref, low_ref, twist_ref,
    low_pos, low_typ, low_snd, upp_pos, upp_typ, upp_snd,
    env_ref, moment_ref, in_h_ref, in_l_ref, desc_h_ref, desc_l_ref, w2_ref, w3_ref,
    charge_ref, charges_ref, wxy_ref, wz_h_ref, wz_l_ref, green_ref,
    out1, in1, out2, in2, out3, in3, out4, in4, modes_ref, pot_ref, part_ref, back_ref,
    load_sem, pot_sem, ghost_send, ghost_recv, cell_send, cell_recv, charge_send, charge_recv,
    part_send, part_recv, send1, recv1, send2, recv2, send3, recv3, send4, recv4,
):
    b = lax.axis_index("brick")
    s = lax.axis_index("slab")
    b_up, b_down = lax.rem(b + 1, NB), lax.rem(b + NB - 1, NB)
    s_up, s_down = lax.rem(s + 1, NS), lax.rem(s + NS - 1, NS)
    below, above = (b_down, s), (b_up, s)
    shifts = ((0, 0), (1, 0), (0, 1), (1, 1))
    onward = ((b, s), (b_up, s), (b, s_up), (b_up, s_up))
    origin = ((b, s), (b_down, s), (b, s_down), (b_down, s_down))

    barrier = pltpu.get_barrier_semaphore()

    def greet_slab(i, carry):
        pl.semaphore_signal(barrier, inc=1, device_id=(b, lax.rem(s + i, NS)), device_id_type=MESH)
        return carry

    def greet_brick(i, carry):
        pl.semaphore_signal(barrier, inc=1, device_id=(lax.rem(b + i, NB), s), device_id_type=MESH)
        return carry

    lax.fori_loop(1, NS, greet_slab, 0)
    lax.fori_loop(1, NB, greet_brick, 0)
    for device in (onward[3], origin[3]):
        pl.semaphore_signal(barrier, inc=1, device_id=device, device_id_type=MESH)

    sources = (
        table_any, first_any, second_any, third_any, e_in_any, w_in_any,
        neigh_any, pos_any, typ_any, count_any,
        e_hid_any, w_hid_any, e_out_any, w_out_any, base_any,
        cx_any, cy_any, cz_any, frac_any, high_any, low_any, twist_any,
    )
    targets = (
        table_ref, first_ref, second_ref, third_ref, e_in_ref, w_in_ref,
        neigh_ref, pos_ref, typ_ref, count_ref,
        e_hid_ref, w_hid_ref, e_out_ref, w_out_ref, base_ref,
        cx_ref.at[0], cy_ref.at[0], cz_ref.at[0], frac_ref.at[0], high_ref, low_ref, twist_ref,
    )
    loads = [
        pltpu.make_async_copy(source, target, load_sem.at[i])
        for i, (source, target) in enumerate(zip(sources, targets, strict=True))
    ]
    for load in loads:
        load.start()

    pl.semaphore_wait(barrier, NS + NB)

    def remote(source, target, send_sem, recv_sem, device):
        return pltpu.make_async_remote_copy(
            src_ref=source, dst_ref=target, send_sem=send_sem, recv_sem=recv_sem,
            device_id=device, device_id_type=MESH,
        )

    plan = (
        (above, pos_any, low_pos), (above, typ_any, low_typ), (above, snd_any, low_snd),
        (below, pos_any, upp_pos), (below, typ_any, upp_typ), (below, snd_any, upp_snd),
    )
    ghosts = [
        remote(source, target, ghost_send.at[i], ghost_recv.at[i], device)
        for i, (device, source, target) in enumerate(plan)
    ]
    for ghost in ghosts:
        ghost.start()
    cells = []
    for n in range(1, 4):
        pairs = ((cx_any, cx_ref), (cy_any, cy_ref), (cz_any, cz_ref), (frac_any, frac_ref))
        for i, (source, target) in enumerate(pairs):
            k = (n - 1) * 4 + i
            cells.append(
                remote(source, target.at[n], cell_send.at[k], cell_recv.at[k], onward[n])
            )
    for cell in cells:
        cell.start()

    row = rows_iota((256, 128))
    lane = lanes_iota((256, 128))

    def kappa(index):
        folded = jnp.minimum(index, NG - index)
        return folded.astype(F32) * (2.0 * math.pi / NG)

    kx = kappa(row // 8 + 32 * (lane // 16))
    ky = kappa(b * 8 + row % 8)
    kz = kappa(s * 16 + lane % 16)
    squared = kx * kx + ky * ky + kz * kz
    root = jnp.where(squared == 0.0, 1.0, 0.0)
    green_ref[...] = (1.0 - root) * jnp.exp(-0.5 * squared) / (squared + root) * (1.0 / NG)

    for load in loads[:4]:
        load.wait()
    f1 = lax.dot_general(table_ref[0:32, 0:25], first_ref[...], NT, precision=HIGHEST)
    oxygen, hydrogen = f1[:, 0:1], f1[:, 1:2]
    w2 = lax.dot_general(table_ref[32:96, 0:50], second_ref[...], NT, precision=HIGHEST)
    w2 = lax.dot_general(w2, table_ref[208:233, 0:96], NN, precision=HIGHEST)
    high, low = halves(w2)
    slot = lanes_iota((64, 96)) // 32
    w2_ref[...] = jnp.where(slot == 1, low.astype(F32), high.astype(F32)).astype(BF16)
    w3 = lax.dot_general(table_ref[96:208, 0:100], third_ref[...], NT, precision=HIGHEST)
    w3 = lax.dot_general(w3, table_ref[240:290, 0:192], NN, precision=HIGHEST)
    high, low = halves(w3)
    slot = lanes_iota((112, 192)) // 64
    w3_ref[...] = jnp.where(slot == 1, low.astype(F32), high.astype(F32)).astype(BF16)

    for load in loads[4:10]:
        load.wait()
    high, low = halves(e_in_ref[...])
    in_h_ref[0:240, :] = high
    in_l_ref[0:240, :] = low
    high, low = halves(w_in_ref[...])
    in_h_ref[240:480, :] = high
    in_l_ref[240:480, :] = low

    n = jnp.concatenate(
        [
            neigh_ref[0, :, 0:128],
            jnp.concatenate([neigh_ref[0, 0:32, 128:192], neigh_ref[0, 32:64, 128:192]], axis=1),
        ],
        axis=0,
    )

    def near(row):
        return row[:, 0:128]

    def far(row):
        return jnp.concatenate([row[:, 128:192], row[:, 128:192]], axis=1)

    def by_atom(row):
        return jnp.concatenate(
            [jnp.broadcast_to(near(row), (64, 128)), jnp.broadcast_to(far(row), (32, 128))], axis=0
        )

    own_index = (n - 96) & 127
    lower_index = n & 127
    upper_index = (n - 288) & 127
    row96 = rows_iota((96, 128))
    slot = jnp.where(row96 < 64, row96, row96 - 64 + jnp.where(lanes_iota((96, 128)) < 64, 0, 32))
    live = slot < by_atom(count_ref[...])

    for ghost in ghosts:
        ghost.wait_recv()

    low_snd_row = low_snd[...]
    upp_snd_row = upp_snd[...]
    low_list = jnp.concatenate([low_snd_row[:, 96:192], low_snd_row[:, 0:32]], axis=1)
    upp_list = upp_snd_row[:, 0:128]

    def ghost_row(row, index):
        index = jnp.broadcast_to(index, (8, 128))
        value = jnp.where(index < 128, pick(near(row), index & 127), pick(far(row), index & 127))
        return value[0:1]

    gathered = []
    for c in range(4):
        own = pos_ref[c] if c < 3 else typ_ref[...].astype(F32)
        low = low_pos[c] if c < 3 else low_typ[...].astype(F32)
        upp = upp_pos[c] if c < 3 else upp_typ[...].astype(F32)
        value = jnp.where(n < 224, pick(near(own), own_index), pick(far(own), own_index))
        value = jnp.where(n < 96, pick(ghost_row(low, low_list), lower_index), value)
        value = jnp.where(n >= 288, pick(ghost_row(upp, upp_list), upper_index), value)
        if c < 3:
            value = value - by_atom(own)
        gathered.append(value)
    squared = gathered[0] * gathered[0] + gathered[1] * gathered[1] + gathered[2] * gathered[2]
    smooth = jnp.where(live, 1.0 / (1.0 + squared), 0.0)
    env_ref[0] = smooth
    for c in range(3):
        env_ref[c + 1] = smooth * gathered[c]
    env_ref[4] = gathered[3]
    moment_ref[...] = jnp.zeros_like(moment_ref)

    oxygen_wide = jnp.broadcast_to(oxygen, (32, 128))
    hydrogen_wide = jnp.broadcast_to(hydrogen, (32, 128))

    def chunk(step, carry):
        at = pl.multiple_of(step * 8, 8)
        tile = step // 8
        first = []
        for r in range(8):
            sm = env_ref[0, pl.ds(at + r, 1), :]
            kind = env_ref[4, pl.ds(at + r, 1), :]
            mixing = jnp.where(kind > 0.5, hydrogen_wide, oxygen_wide)
            first.append(jnp.tanh(sm * mixing))
        first = jnp.concatenate(first, axis=1)
        high, low = halves(first)
        second = dot(w2_ref[...], jnp.concatenate([high, high, low], axis=0))
        second = jnp.tanh(second[:56]) + jnp.concatenate([first[:24], first], axis=0)
        padded = jnp.concatenate([second, jnp.zeros((8, 1024), F32)], axis=0)
        high, low = halves(padded)
        third = dot(w3_ref[...], jnp.concatenate([high, high, low], axis=0))
        third = jnp.tanh(third[:104]) + jnp.concatenate([second[:48], second], axis=0)
        for c in range(4):
            total = None
            for r in range(8):
                part = third[:, r * 128 : (r + 1) * 128] * env_ref[c, pl.ds(at + r, 1), :]
                total = part if total is None else total + part
            moment_ref[tile, c] += total
        return carry

    lax.fori_loop(0, 12, chunk, 0, unroll=4)

    for c in range(4):
        moment_ref[0, c] = moment_ref[0, c] * (1.0 / 64.0)
        value = moment_ref[1, c]
        moment_ref[1, c] = (value + pltpu.roll(value, 64, 1)) * (1.0 / 64.0)
    for tile in range(2):
        factors = [moment_ref[tile, c, 0:16, :] for c in range(4)]
        for m, place in enumerate(places()):
            value = None
            for c in range(4):
                term = moment_ref[tile, c, place : place + 1, :] * factors[c]
                value = term if value is None else value + term
            high, low = halves(value)
            desc_h_ref[m * 16 : m * 16 + 16, tile * 128 : (tile + 1) * 128] = high
            desc_l_ref[m * 16 : m * 16 + 16, tile * 128 : (tile + 1) * 128] = low

    for load in loads[10:]:
        load.wait()

    def network(rows, hid_ref, out_ref):
        weight = in_h_ref[rows, :], in_l_ref[rows, :]
        hidden = jnp.tanh(dot3(weight, (desc_h_ref[...], desc_l_ref[...]))).T
        for layer in range(2):
            hidden = jnp.tanh(dot3(halves(hidden), halves(hid_ref[layer]))) + hidden
        row = jnp.broadcast_to(out_ref[...], (16, 240))
        return dot3(halves(row), halves(hidden), NT)[0:1, 0:A]

    def short_energy():
        energy_ref[...] = network(slice(0, 240), e_hid_ref, e_out_ref)

    shift = network(slice(240, 480), w_hid_ref, w_out_ref)
    charge = jnp.where(typ_ref[...] == 1, base_ref[0:1, 1:2], base_ref[0:1, 0:1]) + shift
    charge_ref[...] = charge
    charges = [
        remote(charge_ref, charges_ref.at[n], charge_send.at[n], charge_recv.at[n], onward[n])
        for n in range(1, 4)
    ]
    for copy in charges:
        copy.start()

    for cell in cells:
        cell.wait_recv()
    grid = None
    for n, (dx, dy) in enumerate(shifts):
        wx = place_rows(cx_ref[n] - dx * CX, spline_rows(frac_ref[n, 0]), CX, 0)
        wy = place_rows(cy_ref[n] - dy * CY, spline_rows(frac_ref[n, 1]), CY, 0)
        high, low = halves(place_rows(cz_ref[n], spline_rows(frac_ref[n, 2]), NG, NG))
        wz_h_ref[n] = high
        wz_l_ref[n] = low
        wxy = jnp.concatenate([wx[x : x + 1] * wy for x in range(CX)], axis=0)
        wxy_ref[n] = wxy
    for n in range(4):
        if n:
            charges[n - 1].wait_recv()
        weighted = wxy_ref[n] * (charges_ref[n] if n else charge)
        part = dot3(halves(weighted), (wz_h_ref[n], wz_l_ref[n]), NT)
        grid = part if grid is None else grid + part

    def table(k, count=1):
        at = slice(k * NG, (k + count) * NG)
        return high_ref[at, :], low_ref[at, :]

    spectrum = dot3(halves(grid), table(0))
    chunk_lane = lanes_iota((CY, 128)) // 16
    for to in range(NS):
        tile, chunk_from = divmod(to, 8)
        out = jnp.zeros((CY, 128), F32)
        for x in range(CX):
            source = spectrum[x * CY : (x + 1) * CY, tile * 128 : (tile + 1) * 128]
            shift_by = 16 * (x - chunk_from) % 128
            if shift_by:
                source = pltpu.roll(source, shift_by, 1)
            out = jnp.where(chunk_lane == x, source, out)
        out1[to] = out

    def exchange(source, target, send_sem, recv_sem, me, count, device_of, meanwhile=None):
        def copy(i):
            to = lax.rem(me + i, count)
            return remote(
                source.at[to], target.at[me], send_sem.at[to], recv_sem.at[me], device_of(to)
            )

        def arrival(i):
            frm = lax.rem(me + count - i, count)
            return remote(
                source.at[frm], target.at[frm], send_sem.at[frm], recv_sem.at[frm], device_of(frm)
            )

        def start(i, carry):
            copy(i).start()
            return carry

        def wait(i, carry):
            arrival(i).wait_recv()
            return carry

        def drain(i, carry):
            copy(i).wait_send()
            return carry

        lax.fori_loop(1, count, start, 0)
        target[me] = source[me]
        if meanwhile is not None:
            meanwhile()
        lax.fori_loop(1, count, wait, 0)
        return lambda: lax.fori_loop(1, count, drain, 0)

    def over_slab(source, target, send_sem, recv_sem, meanwhile=None):
        return exchange(source, target, send_sem, recv_sem, s, NS, lambda to: (b, to), meanwhile)

    def over_brick(source, target, send_sem, recv_sem):
        return exchange(source, target, send_sem, recv_sem, b, NB, lambda to: (to, s))

    drains = [over_slab(out1, in1, send1, recv1, short_energy)]
    data = halves(in1[...].reshape(NG, 128))
    out2[...] = dot3_narrow(table(1), data).reshape(NB, 8, 128)
    drains.append(over_brick(out2, in2, send2, recv2))

    data = halves(in2[...].reshape(NG, 128))
    both = dot3_narrow(table(2, 2), data)
    uc, us = both[:256], both[256:]
    tc, ts = twist_ref[0:256, :], twist_ref[256:512, :]
    turned = jnp.concatenate([uc * tc - us * ts, -(uc * ts + us * tc)], axis=1)
    green = green_ref[...]
    modes = dot3(halves(turned), table(4)) * jnp.concatenate([green, green], axis=1)
    back = dot3(halves(modes), table(4), NT)
    vr, vi = back[:, :128], back[:, 128:]
    real = dot3_narrow(table(2), halves(vr * tc - vi * ts))
    imag = dot3_narrow(table(3), halves(vr * ts + vi * tc))
    out3[...] = (real - imag).reshape(NB, 8, 128)
    drains.append(over_brick(out3, in3, send3, recv3))
    data = halves(in3[...].reshape(NG, 128))
    out4[...] = dot3_narrow(table(0), data).reshape(NS, CY, 128)
    drains.append(over_slab(out4, in4, send4, recv4))

    for x in range(CX):
        for tile in range(2):
            out = jnp.zeros((CY, 128), F32)
            for c in range(8):
                source = in4[8 * tile + c]
                shift_by = 16 * (c - x) % 128
                if shift_by:
                    source = pltpu.roll(source, shift_by, 1)
                out = jnp.where(chunk_lane == c, source, out)
            modes_ref[x * CY : (x + 1) * CY, tile * 128 : (tile + 1) * 128] = out
    potential = dot3(halves(modes_ref[...]), table(0), NT)
    pot_ref[...] = potential.reshape(CX, CY, NG)
    pot_copy = pltpu.make_async_copy(pot_ref, pot_any, pot_sem)
    pot_copy.start()

    data = halves(potential)
    returns = []
    for n in (1, 2, 3, 0):
        sampled = dot3(data, (wz_h_ref[n], wz_l_ref[n]))
        part_ref[n] = jnp.sum(sampled * wxy_ref[n], axis=0, keepdims=True)
        if n:
            copy = remote(part_ref.at[n], back_ref.at[n], part_send.at[n], part_recv.at[n], origin[n])
            copy.start()
            returns.append(copy)
    for drain in drains:
        drain()
    for copy in ghosts + cells + charges:
        copy.wait_send()
    for copy in returns:
        copy.wait_recv()
    at = part_ref[0] + back_ref[1] + back_ref[2] + back_ref[3]
    energy_ref[...] += 0.5 * charge_ref[...] * at
    for copy in returns:
        copy.wait_send()
    pot_copy.wait()


def hand_over(energy_in, pot_in, energy_out, pot_out, energy_ref, pot_ref, sem):
    arriving = [
        pltpu.make_async_copy(energy_in, energy_ref, sem.at[0]),
        pltpu.make_async_copy(pot_in, pot_ref, sem.at[1]),
    ]
    leaving = [
        pltpu.make_async_copy(energy_ref, energy_out, sem.at[2]),
        pltpu.make_async_copy(pot_ref, pot_out, sem.at[3]),
    ]
    for copy in arriving:
        copy.start()
    for first, second in zip(arriving, leaving, strict=True):
        first.wait()
        second.start()
    for copy in leaving:
        copy.wait()


VMEM = pl.BlockSpec(memory_space=pltpu.VMEM)
ANY = pl.BlockSpec(memory_space=pl.ANY)
I32 = jnp.int32


def per_device(
    positions, types, neighbours, neighbour_count, send_index, cell_x, cell_y, cell_z, spline_fraction,
    embed_first, embed_second, embed_third, energy_in, energy_hidden, energy_out,
    wannier_in, wannier_hidden, wannier_out, charge_base,
):
    vmem = pltpu.VMEM
    dma = pltpu.SemaphoreType.DMA
    slab_block, brick_block = vmem((NS, CY, 128), F32), vmem((NB, 8, 128), F32)
    outs = (jax.ShapeDtypeStruct((1, A), F32), jax.ShapeDtypeStruct((CX, CY, NG), F32))
    results = tuple(
        pl.pallas_call(
            kernel,
            out_shape=outs,
            in_specs=[ANY] * 23,
            out_specs=(VMEM, ANY),
            scratch_shapes=[
                vmem((3, 1, A), F32), vmem((1, A), I32), vmem((1, 64, A), I32), vmem((1, A), I32),
                vmem((4, 1, A), I32), vmem((4, 1, A), I32), vmem((4, 1, A), I32), vmem((4, 3, 1, A), F32),
                vmem((2, 25), F32), vmem((25, 50), F32), vmem((50, 100), F32),
                vmem((240, 1600), F32), vmem((2, 240, 240), F32), vmem((1, 240), F32),
                vmem((240, 1600), F32), vmem((2, 240, 240), F32), vmem((1, 240), F32),
                vmem((1, 2), F32), vmem((296, 256), F32),
                vmem((5 * NG, NG), BF16), vmem((5 * NG, NG), BF16), vmem((2 * NG, 128), F32),
                vmem((3, 1, A), F32), vmem((1, A), I32), vmem((1, A), I32),
                vmem((3, 1, A), F32), vmem((1, A), I32), vmem((1, A), I32),
                vmem((5, 96, 128), F32), vmem((2, 4, 104, 128), F32),
                vmem((480, 1600), BF16), vmem((480, 1600), BF16),
                vmem((1600, 256), BF16), vmem((1600, 256), BF16),
                vmem((64, 96), BF16), vmem((112, 192), BF16),
                vmem((1, A), F32), vmem((4, 1, A), F32), vmem((4, 128, A), F32),
                vmem((4, NG, A), BF16), vmem((4, NG, A), BF16), vmem((NG, 128), F32),
                slab_block, slab_block, brick_block, brick_block,
                brick_block, brick_block, slab_block, slab_block,
                vmem((128, NG), F32), vmem((CX, CY, NG), F32), vmem((4, 1, A), F32), vmem((4, 1, A), F32),
                dma((LOADED,)), dma, dma((6,)), dma((6,)), dma((12,)), dma((12,)), dma((4,)), dma((4,)),
                dma((4,)), dma((4,)), dma((NS,)), dma((NS,)), dma((NB,)), dma((NB,)),
                dma((NB,)), dma((NB,)), dma((NS,)), dma((NS,)),
            ],
            compiler_params=pltpu.CompilerParams(
                collective_id=1, has_side_effects=True, vmem_limit_bytes=60 * MIB
            ),
            name="potential",
        )(
            positions, types, send_index, jnp.swapaxes(neighbours, 1, 2), neighbour_count,
            cell_x, cell_y, cell_z, spline_fraction,
            embed_first, embed_second, embed_third,
            energy_in.T, energy_hidden, energy_out.reshape(1, -1),
            wannier_in.T, wannier_hidden, wannier_out.reshape(1, -1), charge_base.reshape(1, 2),
            embedding_tables(), *transform_tables(),
        )
    )
    return pl.pallas_call(
        hand_over,
        out_shape=outs,
        in_specs=[ANY, ANY],
        out_specs=(ANY, ANY),
        scratch_shapes=[vmem((1, A), F32), vmem((CX, CY, NG), F32), dma((4,))],
        compiler_params=pltpu.CompilerParams(vmem_limit_bytes=60 * MIB),
        name="hand_over",
    )(*results)


def solution(mesh):
    row = P("slab", "brick")
    three = P(None, "slab", "brick")
    placed = (three, row, P("slab", "brick", None), row, row, row, row, row, three) + (P(),) * 10
    return jax.shard_map(
        per_device,
        mesh=mesh,
        in_specs=placed,
        out_specs=(row, P("brick", "slab", None)),
        check_vma=False,
    )
```

```python
import math

import jax
import jax.numpy as jnp
import numpy as np
from jax import lax
from jax.experimental import pallas as pl
from jax.experimental.pallas import tpu as pltpu
from jax.sharding import PartitionSpec as P

NG = 256
A = 192
NB = 32
NS = 16
CX = 8
CY = 16
MIB = 1024 * 1024
F32 = jnp.float32
BF16 = jnp.bfloat16
HIGHEST = lax.Precision.HIGHEST
MESH = pl.DeviceIdType.MESH

NN = (((1,), (0,)), ((), ()))
NT = (((1,), (1,)), ((), ()))


def split(table):
    table = np.asarray(table, np.float64)
    high = np.asarray(table, np.float32).astype(jnp.bfloat16)
    low = (table - high.astype(np.float64)).astype(np.float32).astype(jnp.bfloat16)
    return high, low


def real_basis():
    n = np.arange(NG)[:, None]
    j = np.arange(NG)[None, :]
    phase = 2.0 * np.pi * ((n * j) % NG) / NG
    basis = np.where(j <= NG // 2, np.cos(phase), np.sin(phase)) * math.sqrt(2.0 / NG)
    basis[:, 0] = 1.0 / 16.0
    basis[:, NG // 2] = np.where(np.arange(NG) % 2 == 0, 1.0, -1.0) / 16.0
    return basis


def transform_tables():
    basis = real_basis()
    b = np.arange(NB)
    angle = 2.0 * np.pi * np.outer(b, b) / NB
    eye8 = np.eye(8)
    left = np.concatenate([np.kron(np.cos(angle), eye8), np.kron(np.sin(angle), eye8)], axis=0)
    xi = np.arange(8)
    small = 2.0 * np.pi * np.outer(xi, xi) / 8
    eye16 = np.eye(16)
    cos_m = np.kron(np.cos(small), eye16)
    sin_m = np.kron(np.sin(small), eye16)
    right = np.block([[cos_m, -sin_m], [sin_m, cos_m]])
    high, low = zip(*(split(table) for table in (basis, basis.T, left, right)), strict=True)
    twist = 2.0 * np.pi * np.repeat(b, 8)[:, None] * np.repeat(xi, 16)[None, :] / NG
    twist = np.concatenate([np.cos(twist), np.sin(twist)]).astype(np.float32)
    return np.concatenate(high), np.concatenate(low), twist


def second_rows():
    rows = list(range(24)) + list(range(25, 49)) + [24, 49, 24, 49]
    return rows


def third_rows():
    second = second_rows()
    return [f for f in second[:48]] + [50 + f for f in second[:48]] + [24, 49, 74, 99]


def one_hot(rows, height, width):
    table = np.zeros((height, width), np.float32)
    for row, feature in enumerate(rows):
        table[row, feature] = 1.0
    return table


def embedding_tables():
    first = one_hot(list(range(25)) + [24, 24, 24], 32, 25)
    second = one_hot(second_rows(), 64, 50)
    third = one_hot(third_rows(), 112, 100)
    columns_first = np.tile(np.eye(25, 32, dtype=np.float32), (1, 3))
    placed = np.zeros((50, 64), np.float32)
    for row, feature in enumerate(second_rows()[:50]):
        placed[feature, row] = 1.0
    columns_second = np.tile(placed, (1, 3))
    table = np.zeros((296, 256), np.float32)
    table[0:32, :25] = first
    table[32:96, :50] = second
    table[96:208, :100] = third
    table[208:233, :96] = columns_first
    table[240:290, :192] = columns_second
    return table


def places():
    rows = third_rows()
    return [rows.index(feature) for feature in range(100)]


def halves(values):
    high = values.astype(BF16)
    low = (values - high.astype(F32)).astype(BF16)
    return high, low


def dot(a, b, dims=NN):
    return lax.dot_general(a, b, dims, preferred_element_type=F32)


def dot3(a, b, dims=NN):
    return dot(a[0], b[0], dims) + (dot(a[0], b[1], dims) + dot(a[1], b[0], dims))


def dot3_narrow(a, b):
    both = dot(a[0], jnp.concatenate([b[0], b[1]], axis=1))
    return both[:, :128] + (both[:, 128:] + dot(a[1], b[0]))


def lanes_iota(shape):
    return lax.broadcasted_iota(jnp.int32, shape, 1)


def rows_iota(shape):
    return lax.broadcasted_iota(jnp.int32, shape, 0)


def pick(row, index):
    table = jnp.broadcast_to(row, index.shape)
    return jnp.take_along_axis(table, index, axis=1, mode="promise_in_bounds")


def spline_rows(u):
    cubed = u * u * u
    square = u * u
    rest = 1.0 - u
    return (
        rest * rest * rest / 6.0,
        (3.0 * cubed - 6.0 * square + 4.0) / 6.0,
        (-3.0 * cubed + 3.0 * square + 3.0 * u + 1.0) / 6.0,
        cubed / 6.0,
    )


def place_rows(start, weights, height, wrap):
    offset = rows_iota((height, A)) - start
    if wrap:
        offset = offset & (wrap - 1)
    result = jnp.zeros((height, A), F32)
    for step in range(4):
        result = jnp.where(offset == step, weights[step], result)
    return result


LOADED = 22


def kernel(
    pos_any, typ_any, snd_any, neigh_any, count_any, cx_any, cy_any, cz_any, frac_any,
    first_any, second_any, third_any, e_in_any, e_hid_any, e_out_any, w_in_any, w_hid_any, w_out_any,
    base_any, table_any, high_any, low_any, twist_any,
    energy_ref, pot_any,
    pos_ref, typ_ref, neigh_ref, count_ref, cx_ref, cy_ref, cz_ref, frac_ref,
    first_ref, second_ref, third_ref, e_in_ref, e_hid_ref, e_out_ref, w_in_ref, w_hid_ref, w_out_ref,
    base_ref, table_ref, high_ref, low_ref, twist_ref,
    low_pos, low_typ, low_snd, upp_pos, upp_typ, upp_snd,
    env_ref, moment_ref, in_h_ref, in_l_ref, desc_h_ref, desc_l_ref, w2_ref, w3_ref,
    charge_ref, charges_ref, wxy_ref, wz_h_ref, wz_l_ref, green_ref,
    out1, in1, out2, in2, out3, in3, out4, in4, modes_ref, pot_ref, part_ref, back_ref,
    load_sem, pot_sem, ghost_send, ghost_recv, cell_send, cell_recv, charge_send, charge_recv,
    part_send, part_recv, send1, recv1, send2, recv2, send3, recv3, send4, recv4,
):
    b = lax.axis_index("brick")
    s = lax.axis_index("slab")
    b_up, b_down = lax.rem(b + 1, NB), lax.rem(b + NB - 1, NB)
    s_up, s_down = lax.rem(s + 1, NS), lax.rem(s + NS - 1, NS)
    below, above = (b_down, s), (b_up, s)
    shifts = ((0, 0), (1, 0), (0, 1), (1, 1))
    onward = ((b, s), (b_up, s), (b, s_up), (b_up, s_up))
    origin = ((b, s), (b_down, s), (b, s_down), (b_down, s_down))

    barrier = pltpu.get_barrier_semaphore()

    def greet_slab(i, carry):
        pl.semaphore_signal(barrier, inc=1, device_id=(b, lax.rem(s + i, NS)), device_id_type=MESH)
        return carry

    def greet_brick(i, carry):
        pl.semaphore_signal(barrier, inc=1, device_id=(lax.rem(b + i, NB), s), device_id_type=MESH)
        return carry

    lax.fori_loop(1, NS, greet_slab, 0)
    lax.fori_loop(1, NB, greet_brick, 0)
    for device in (onward[3], origin[3]):
        pl.semaphore_signal(barrier, inc=1, device_id=device, device_id_type=MESH)

    sources = (
        table_any, first_any, second_any, third_any, e_in_any, w_in_any,
        neigh_any, pos_any, typ_any, count_any,
        e_hid_any, w_hid_any, e_out_any, w_out_any, base_any,
        cx_any, cy_any, cz_any, frac_any, high_any, low_any, twist_any,
    )
    targets = (
        table_ref, first_ref, second_ref, third_ref, e_in_ref, w_in_ref,
        neigh_ref, pos_ref, typ_ref, count_ref,
        e_hid_ref, w_hid_ref, e_out_ref, w_out_ref, base_ref,
        cx_ref.at[0], cy_ref.at[0], cz_ref.at[0], frac_ref.at[0], high_ref, low_ref, twist_ref,
    )
    loads = [
        pltpu.make_async_copy(source, target, load_sem.at[i])
        for i, (source, target) in enumerate(zip(sources, targets, strict=True))
    ]
    for load in loads:
        load.start()

    pl.semaphore_wait(barrier, NS + NB)

    def remote(source, target, send_sem, recv_sem, device):
        return pltpu.make_async_remote_copy(
            src_ref=source, dst_ref=target, send_sem=send_sem, recv_sem=recv_sem,
            device_id=device, device_id_type=MESH,
        )

    plan = (
        (above, pos_any, low_pos), (above, typ_any, low_typ), (above, snd_any, low_snd),
        (below, pos_any, upp_pos), (below, typ_any, upp_typ), (below, snd_any, upp_snd),
    )
    ghosts = [
        remote(source, target, ghost_send.at[i], ghost_recv.at[i], device)
        for i, (device, source, target) in enumerate(plan)
    ]
    for ghost in ghosts:
        ghost.start()
    cells = []
    for n in range(1, 4):
        pairs = ((cx_any, cx_ref), (cy_any, cy_ref), (cz_any, cz_ref), (frac_any, frac_ref))
        for i, (source, target) in enumerate(pairs):
            k = (n - 1) * 4 + i
            cells.append(
                remote(source, target.at[n], cell_send.at[k], cell_recv.at[k], onward[n])
            )
    for cell in cells:
        cell.start()

    row = rows_iota((256, 128))
    lane = lanes_iota((256, 128))

    def kappa(index):
        folded = jnp.minimum(index, NG - index)
        return folded.astype(F32) * (2.0 * math.pi / NG)

    kx = kappa(row // 8 + 32 * (lane // 16))
    ky = kappa(b * 8 + row % 8)
    kz = kappa(s * 16 + lane % 16)
    squared = kx * kx + ky * ky + kz * kz
    root = jnp.where(squared == 0.0, 1.0, 0.0)
    green_ref[...] = (1.0 - root) * jnp.exp(-0.5 * squared) / (squared + root) * (1.0 / NG)

    for load in loads[:4]:
        load.wait()
    f1 = lax.dot_general(table_ref[0:32, 0:25], first_ref[...], NT, precision=HIGHEST)
    oxygen, hydrogen = f1[:, 0:1], f1[:, 1:2]
    w2 = lax.dot_general(table_ref[32:96, 0:50], second_ref[...], NT, precision=HIGHEST)
    w2 = lax.dot_general(w2, table_ref[208:233, 0:96], NN, precision=HIGHEST)
    high, low = halves(w2)
    slot = lanes_iota((64, 96)) // 32
    w2_ref[...] = jnp.where(slot == 1, low.astype(F32), high.astype(F32)).astype(BF16)
    w3 = lax.dot_general(table_ref[96:208, 0:100], third_ref[...], NT, precision=HIGHEST)
    w3 = lax.dot_general(w3, table_ref[240:290, 0:192], NN, precision=HIGHEST)
    high, low = halves(w3)
    slot = lanes_iota((112, 192)) // 64
    w3_ref[...] = jnp.where(slot == 1, low.astype(F32), high.astype(F32)).astype(BF16)

    for load in loads[4:10]:
        load.wait()
    high, low = halves(e_in_ref[...])
    in_h_ref[0:240, :] = high
    in_l_ref[0:240, :] = low
    high, low = halves(w_in_ref[...])
    in_h_ref[240:480, :] = high
    in_l_ref[240:480, :] = low

    n = jnp.concatenate(
        [
            neigh_ref[0, :, 0:128],
            jnp.concatenate([neigh_ref[0, 0:32, 128:192], neigh_ref[0, 32:64, 128:192]], axis=1),
        ],
        axis=0,
    )

    def near(row):
        return row[:, 0:128]

    def far(row):
        return jnp.concatenate([row[:, 128:192], row[:, 128:192]], axis=1)

    def by_atom(row):
        return jnp.concatenate(
            [jnp.broadcast_to(near(row), (64, 128)), jnp.broadcast_to(far(row), (32, 128))], axis=0
        )

    own_index = (n - 96) & 127
    lower_index = n & 127
    upper_index = (n - 288) & 127
    row96 = rows_iota((96, 128))
    slot = jnp.where(row96 < 64, row96, row96 - 64 + jnp.where(lanes_iota((96, 128)) < 64, 0, 32))
    live = slot < by_atom(count_ref[...])

    for ghost in ghosts:
        ghost.wait_recv()

    low_snd_row = low_snd[...]
    upp_snd_row = upp_snd[...]
    low_list = jnp.concatenate([low_snd_row[:, 96:192], low_snd_row[:, 0:32]], axis=1)
    upp_list = upp_snd_row[:, 0:128]

    def ghost_row(row, index):
        index = jnp.broadcast_to(index, (8, 128))
        value = jnp.where(index < 128, pick(near(row), index & 127), pick(far(row), index & 127))
        return value[0:1]

    gathered = []
    for c in range(4):
        own = pos_ref[c] if c < 3 else typ_ref[...].astype(F32)
        low = low_pos[c] if c < 3 else low_typ[...].astype(F32)
        upp = upp_pos[c] if c < 3 else upp_typ[...].astype(F32)
        value = jnp.where(n < 224, pick(near(own), own_index), pick(far(own), own_index))
        value = jnp.where(n < 96, pick(ghost_row(low, low_list), lower_index), value)
        value = jnp.where(n >= 288, pick(ghost_row(upp, upp_list), upper_index), value)
        if c < 3:
            value = value - by_atom(own)
        gathered.append(value)
    squared = gathered[0] * gathered[0] + gathered[1] * gathered[1] + gathered[2] * gathered[2]
    smooth = jnp.where(live, 1.0 / (1.0 + squared), 0.0)
    env_ref[0] = smooth
    for c in range(3):
        env_ref[c + 1] = smooth * gathered[c]
    env_ref[4] = gathered[3]
    moment_ref[...] = jnp.zeros_like(moment_ref)

    oxygen_wide = jnp.broadcast_to(oxygen, (32, 128))
    hydrogen_wide = jnp.broadcast_to(hydrogen, (32, 128))

    def chunk(step, carry):
        at = pl.multiple_of(step * 8, 8)
        tile = step // 8
        first = []
        for r in range(8):
            sm = env_ref[0, pl.ds(at + r, 1), :]
            kind = env_ref[4, pl.ds(at + r, 1), :]
            mixing = jnp.where(kind > 0.5, hydrogen_wide, oxygen_wide)
            first.append(jnp.tanh(sm * mixing))
        first = jnp.concatenate(first, axis=1)
        high, low = halves(first)
        second = dot(w2_ref[...], jnp.concatenate([high, high, low], axis=0))
        second = jnp.tanh(second[:56]) + jnp.concatenate([first[:24], first], axis=0)
        padded = jnp.concatenate([second, jnp.zeros((8, 1024), F32)], axis=0)
        high, low = halves(padded)
        third = dot(w3_ref[...], jnp.concatenate([high, high, low], axis=0))
        third = jnp.tanh(third[:104]) + jnp.concatenate([second[:48], second], axis=0)
        for c in range(4):
            total = None
            for r in range(8):
                part = third[:, r * 128 : (r + 1) * 128] * env_ref[c, pl.ds(at + r, 1), :]
                total = part if total is None else total + part
            moment_ref[tile, c] += total
        return carry

    lax.fori_loop(0, 12, chunk, 0, unroll=4)

    for c in range(4):
        moment_ref[0, c] = moment_ref[0, c] * (1.0 / 64.0)
        value = moment_ref[1, c]
        moment_ref[1, c] = (value + pltpu.roll(value, 64, 1)) * (1.0 / 64.0)
    for tile in range(2):
        factors = [moment_ref[tile, c, 0:16, :] for c in range(4)]
        for m, place in enumerate(places()):
            value = None
            for c in range(4):
                term = moment_ref[tile, c, place : place + 1, :] * factors[c]
                value = term if value is None else value + term
            high, low = halves(value)
            desc_h_ref[m * 16 : m * 16 + 16, tile * 128 : (tile + 1) * 128] = high
            desc_l_ref[m * 16 : m * 16 + 16, tile * 128 : (tile + 1) * 128] = low

    for load in loads[10:]:
        load.wait()

    def network(rows, hid_ref, out_ref):
        weight = in_h_ref[rows, :], in_l_ref[rows, :]
        hidden = jnp.tanh(dot3(weight, (desc_h_ref[...], desc_l_ref[...]))).T
        for layer in range(2):
            hidden = jnp.tanh(dot3(halves(hidden), halves(hid_ref[layer]))) + hidden
        row = jnp.broadcast_to(out_ref[...], (16, 240))
        return dot3(halves(row), halves(hidden), NT)[0:1, 0:A]

    def short_energy():
        energy_ref[...] = network(slice(0, 240), e_hid_ref, e_out_ref)

    shift = network(slice(240, 480), w_hid_ref, w_out_ref)
    charge = jnp.where(typ_ref[...] == 1, base_ref[0:1, 1:2], base_ref[0:1, 0:1]) + shift
    charge_ref[...] = charge
    charges = [
        remote(charge_ref, charges_ref.at[n], charge_send.at[n], charge_recv.at[n], onward[n])
        for n in range(1, 4)
    ]
    for copy in reversed(charges):
        copy.start()

    for cell in cells:
        cell.wait_recv()
    grid = None
    for n, (dx, dy) in enumerate(shifts):
        wx = place_rows(cx_ref[n] - dx * CX, spline_rows(frac_ref[n, 0]), CX, 0)
        wy = place_rows(cy_ref[n] - dy * CY, spline_rows(frac_ref[n, 1]), CY, 0)
        high, low = halves(place_rows(cz_ref[n], spline_rows(frac_ref[n, 2]), NG, NG))
        wz_h_ref[n] = high
        wz_l_ref[n] = low
        wxy = jnp.concatenate([wx[x : x + 1] * wy for x in range(CX)], axis=0)
        wxy_ref[n] = wxy
    for n in range(4):
        if n:
            charges[n - 1].wait_recv()
        weighted = wxy_ref[n] * (charges_ref[n] if n else charge)
        part = dot3(halves(weighted), (wz_h_ref[n], wz_l_ref[n]), NT)
        grid = part if grid is None else grid + part

    def table(k, count=1):
        at = slice(k * NG, (k + count) * NG)
        return high_ref[at, :], low_ref[at, :]

    spectrum = dot3(halves(grid), table(0))
    chunk_lane = lanes_iota((CY, 128)) // 16
    for to in range(NS):
        tile, chunk_from = divmod(to, 8)
        out = jnp.zeros((CY, 128), F32)
        for x in range(CX):
            source = spectrum[x * CY : (x + 1) * CY, tile * 128 : (tile + 1) * 128]
            shift_by = 16 * (x - chunk_from) % 128
            if shift_by:
                source = pltpu.roll(source, shift_by, 1)
            out = jnp.where(chunk_lane == x, source, out)
        out1[to] = out

    def exchange(source, target, send_sem, recv_sem, me, peers, device_of, meanwhile=None):
        copies = [
            remote(source.at[k], target.at[me], send_sem.at[k], recv_sem.at[me], device_of(k))
            for k in peers
        ]
        for copy in copies:
            copy.start()
        target[me] = source[me]
        if meanwhile is not None:
            meanwhile()
        for k in peers:
            remote(
                source.at[k], target.at[k], send_sem.at[k], recv_sem.at[k], device_of(k)
            ).wait_recv()
        return copies

    far_first = (4, 5, 3, 6, 2, 7, 1)
    turns = [(1, d) for d in (*far_first, 0)] + [(0, d) for d in far_first]
    slabs = [lax.rem(s // 8 + half, 2) * 8 + lax.rem(s + d, 8) for half, d in turns]
    turns = [(x, d) for x in (2, 1, 3) for d in (*far_first, 0)] + [(0, d) for d in far_first]
    bricks = [lax.rem(b // 8 + x, 4) * 8 + lax.rem(b + d, 8) for x, d in turns]

    def over_slab(source, target, send_sem, recv_sem, meanwhile=None):
        return exchange(
            source, target, send_sem, recv_sem, s, slabs, lambda to: (b, to), meanwhile
        )

    def over_brick(source, target, send_sem, recv_sem):
        return exchange(source, target, send_sem, recv_sem, b, bricks, lambda to: (to, s))

    sent = over_slab(out1, in1, send1, recv1, short_energy)
    data = halves(in1[...].reshape(NG, 128))
    out2[...] = dot3_narrow(table(1), data).reshape(NB, 8, 128)
    sent += over_brick(out2, in2, send2, recv2)

    data = halves(in2[...].reshape(NG, 128))
    both = dot3_narrow(table(2, 2), data)
    uc, us = both[:256], both[256:]
    tc, ts = twist_ref[0:256, :], twist_ref[256:512, :]
    turned = jnp.concatenate([uc * tc - us * ts, -(uc * ts + us * tc)], axis=1)
    green = green_ref[...]
    modes = dot3(halves(turned), table(4)) * jnp.concatenate([green, green], axis=1)
    back = dot3(halves(modes), table(4), NT)
    vr, vi = back[:, :128], back[:, 128:]
    real = dot3_narrow(table(2), halves(vr * tc - vi * ts))
    imag = dot3_narrow(table(3), halves(vr * ts + vi * tc))
    out3[...] = (real - imag).reshape(NB, 8, 128)
    sent += over_brick(out3, in3, send3, recv3)
    data = halves(in3[...].reshape(NG, 128))
    out4[...] = dot3_narrow(table(0), data).reshape(NS, CY, 128)
    sent += over_slab(out4, in4, send4, recv4)

    for x in range(CX):
        for tile in range(2):
            out = jnp.zeros((CY, 128), F32)
            for c in range(8):
                source = in4[8 * tile + c]
                shift_by = 16 * (c - x) % 128
                if shift_by:
                    source = pltpu.roll(source, shift_by, 1)
                out = jnp.where(chunk_lane == c, source, out)
            modes_ref[x * CY : (x + 1) * CY, tile * 128 : (tile + 1) * 128] = out
    potential = dot3(halves(modes_ref[...]), table(0), NT)
    pot_ref[...] = potential.reshape(CX, CY, NG)
    pot_copy = pltpu.make_async_copy(pot_ref, pot_any, pot_sem)
    pot_copy.start()

    data = halves(potential)
    returns = []
    for n in (3, 1, 2, 0):
        sampled = dot3(data, (wz_h_ref[n], wz_l_ref[n]))
        part_ref[n] = jnp.sum(sampled * wxy_ref[n], axis=0, keepdims=True)
        if n:
            copy = remote(part_ref.at[n], back_ref.at[n], part_send.at[n], part_recv.at[n], origin[n])
            copy.start()
            returns.append(copy)
    for copy in sent + ghosts + cells + charges:
        copy.wait_send()
    for copy in returns:
        copy.wait_recv()
    at = part_ref[0] + back_ref[1] + back_ref[2] + back_ref[3]
    energy_ref[...] += 0.5 * charge_ref[...] * at
    for copy in returns:
        copy.wait_send()
    pot_copy.wait()


def hand_over(energy_in, pot_in, energy_out, pot_out, energy_ref, pot_ref, sem):
    arriving = [
        pltpu.make_async_copy(energy_in, energy_ref, sem.at[0]),
        pltpu.make_async_copy(pot_in, pot_ref, sem.at[1]),
    ]
    leaving = [
        pltpu.make_async_copy(energy_ref, energy_out, sem.at[2]),
        pltpu.make_async_copy(pot_ref, pot_out, sem.at[3]),
    ]
    for copy in arriving:
        copy.start()
    for first, second in zip(arriving, leaving, strict=True):
        first.wait()
        second.start()
    for copy in leaving:
        copy.wait()


VMEM = pl.BlockSpec(memory_space=pltpu.VMEM)
ANY = pl.BlockSpec(memory_space=pl.ANY)
I32 = jnp.int32


def per_device(
    positions, types, neighbours, neighbour_count, send_index, cell_x, cell_y, cell_z, spline_fraction,
    embed_first, embed_second, embed_third, energy_in, energy_hidden, energy_out,
    wannier_in, wannier_hidden, wannier_out, charge_base,
):
    vmem = pltpu.VMEM
    dma = pltpu.SemaphoreType.DMA
    slab_block, brick_block = vmem((NS, CY, 128), F32), vmem((NB, 8, 128), F32)
    outs = (jax.ShapeDtypeStruct((1, A), F32), jax.ShapeDtypeStruct((CX, CY, NG), F32))
    results = tuple(
        pl.pallas_call(
            kernel,
            out_shape=outs,
            in_specs=[ANY] * 23,
            out_specs=(VMEM, ANY),
            scratch_shapes=[
                vmem((3, 1, A), F32), vmem((1, A), I32), vmem((1, 64, A), I32), vmem((1, A), I32),
                vmem((4, 1, A), I32), vmem((4, 1, A), I32), vmem((4, 1, A), I32), vmem((4, 3, 1, A), F32),
                vmem((2, 25), F32), vmem((25, 50), F32), vmem((50, 100), F32),
                vmem((240, 1600), F32), vmem((2, 240, 240), F32), vmem((1, 240), F32),
                vmem((240, 1600), F32), vmem((2, 240, 240), F32), vmem((1, 240), F32),
                vmem((1, 2), F32), vmem((296, 256), F32),
                vmem((5 * NG, NG), BF16), vmem((5 * NG, NG), BF16), vmem((2 * NG, 128), F32),
                vmem((3, 1, A), F32), vmem((1, A), I32), vmem((1, A), I32),
                vmem((3, 1, A), F32), vmem((1, A), I32), vmem((1, A), I32),
                vmem((5, 96, 128), F32), vmem((2, 4, 104, 128), F32),
                vmem((480, 1600), BF16), vmem((480, 1600), BF16),
                vmem((1600, 256), BF16), vmem((1600, 256), BF16),
                vmem((64, 96), BF16), vmem((112, 192), BF16),
                vmem((1, A), F32), vmem((4, 1, A), F32), vmem((4, 128, A), F32),
                vmem((4, NG, A), BF16), vmem((4, NG, A), BF16), vmem((NG, 128), F32),
                slab_block, slab_block, brick_block, brick_block,
                brick_block, brick_block, slab_block, slab_block,
                vmem((128, NG), F32), vmem((CX, CY, NG), F32), vmem((4, 1, A), F32), vmem((4, 1, A), F32),
                dma((LOADED,)), dma, dma((6,)), dma((6,)), dma((12,)), dma((12,)), dma((4,)), dma((4,)),
                dma((4,)), dma((4,)), dma((NS,)), dma((NS,)), dma((NB,)), dma((NB,)),
                dma((NB,)), dma((NB,)), dma((NS,)), dma((NS,)),
            ],
            compiler_params=pltpu.CompilerParams(
                collective_id=1, has_side_effects=True, vmem_limit_bytes=60 * MIB
            ),
            name="potential",
        )(
            positions, types, send_index, jnp.swapaxes(neighbours, 1, 2), neighbour_count,
            cell_x, cell_y, cell_z, spline_fraction,
            embed_first, embed_second, embed_third,
            energy_in.T, energy_hidden, energy_out.reshape(1, -1),
            wannier_in.T, wannier_hidden, wannier_out.reshape(1, -1), charge_base.reshape(1, 2),
            embedding_tables(), *transform_tables(),
        )
    )
    return pl.pallas_call(
        hand_over,
        out_shape=outs,
        in_specs=[ANY, ANY],
        out_specs=(ANY, ANY),
        scratch_shapes=[vmem((1, A), F32), vmem((CX, CY, NG), F32), dma((4,))],
        compiler_params=pltpu.CompilerParams(vmem_limit_bytes=60 * MIB),
        name="hand_over",
    )(*results)


def solution(mesh):
    row = P("slab", "brick")
    three = P(None, "slab", "brick")
    placed = (three, row, P("slab", "brick", None), row, row, row, row, row, three) + (P(),) * 10
    return jax.shard_map(
        per_device,
        mesh=mesh,
        in_specs=placed,
        out_specs=(row, P("brick", "slab", None)),
        check_vma=False,
    )
```

```python
import math

import jax
import jax.numpy as jnp
import numpy as np
from jax import lax
from jax.experimental import pallas as pl
from jax.experimental.pallas import tpu as pltpu
from jax.sharding import PartitionSpec as P

NG = 256
A = 192
NB = 32
NS = 16
CX = 8
CY = 16
MIB = 1024 * 1024
F32 = jnp.float32
BF16 = jnp.bfloat16
HIGHEST = lax.Precision.HIGHEST
MESH = pl.DeviceIdType.MESH

NN = (((1,), (0,)), ((), ()))
NT = (((1,), (1,)), ((), ()))


def split(table):
    table = np.asarray(table, np.float64)
    high = np.asarray(table, np.float32).astype(jnp.bfloat16)
    low = (table - high.astype(np.float64)).astype(np.float32).astype(jnp.bfloat16)
    return high, low


def real_basis():
    n = np.arange(NG)[:, None]
    j = np.arange(NG)[None, :]
    phase = 2.0 * np.pi * ((n * j) % NG) / NG
    basis = np.where(j <= NG // 2, np.cos(phase), np.sin(phase)) * math.sqrt(2.0 / NG)
    basis[:, 0] = 1.0 / 16.0
    basis[:, NG // 2] = np.where(np.arange(NG) % 2 == 0, 1.0, -1.0) / 16.0
    return basis


def transform_tables():
    basis = real_basis()
    b = np.arange(NB)
    angle = 2.0 * np.pi * np.outer(b, b) / NB
    eye8 = np.eye(8)
    left = np.concatenate([np.kron(np.cos(angle), eye8), np.kron(np.sin(angle), eye8)], axis=0)
    xi = np.arange(8)
    small = 2.0 * np.pi * np.outer(xi, xi) / 8
    eye16 = np.eye(16)
    cos_m = np.kron(np.cos(small), eye16)
    sin_m = np.kron(np.sin(small), eye16)
    right = np.block([[cos_m, -sin_m], [sin_m, cos_m]])
    high, low = zip(*(split(table) for table in (basis, basis.T, left, right)), strict=True)
    twist = 2.0 * np.pi * np.repeat(b, 8)[:, None] * np.repeat(xi, 16)[None, :] / NG
    twist = np.concatenate([np.cos(twist), np.sin(twist)]).astype(np.float32)
    return np.concatenate(high), np.concatenate(low), twist


def second_rows():
    rows = list(range(24)) + list(range(25, 49)) + [24, 49, 24, 49]
    return rows


def third_rows():
    second = second_rows()
    return [f for f in second[:48]] + [50 + f for f in second[:48]] + [24, 49, 74, 99]


def one_hot(rows, height, width):
    table = np.zeros((height, width), np.float32)
    for row, feature in enumerate(rows):
        table[row, feature] = 1.0
    return table


def embedding_tables():
    first = one_hot(list(range(25)) + [24, 24, 24], 32, 25)
    second = one_hot(second_rows(), 64, 50)
    third = one_hot(third_rows(), 112, 100)
    columns_first = np.tile(np.eye(25, 32, dtype=np.float32), (1, 3))
    placed = np.zeros((50, 64), np.float32)
    for row, feature in enumerate(second_rows()[:50]):
        placed[feature, row] = 1.0
    columns_second = np.tile(placed, (1, 3))
    table = np.zeros((296, 256), np.float32)
    table[0:32, :25] = first
    table[32:96, :50] = second
    table[96:208, :100] = third
    table[208:233, :96] = columns_first
    table[240:290, :192] = columns_second
    return table


def places():
    rows = third_rows()
    return [rows.index(feature) for feature in range(100)]


def halves(values):
    high = values.astype(BF16)
    low = (values - high.astype(F32)).astype(BF16)
    return high, low


def dot(a, b, dims=NN):
    return lax.dot_general(a, b, dims, preferred_element_type=F32)


def dot3(a, b, dims=NN):
    return dot(a[0], b[0], dims) + (dot(a[0], b[1], dims) + dot(a[1], b[0], dims))


def dot3_narrow(a, b):
    both = dot(a[0], jnp.concatenate([b[0], b[1]], axis=1))
    return both[:, :128] + (both[:, 128:] + dot(a[1], b[0]))


def lanes_iota(shape):
    return lax.broadcasted_iota(jnp.int32, shape, 1)


def rows_iota(shape):
    return lax.broadcasted_iota(jnp.int32, shape, 0)


def pick(row, index):
    table = jnp.broadcast_to(row, index.shape)
    return jnp.take_along_axis(table, index, axis=1, mode="promise_in_bounds")


def spline_rows(u):
    cubed = u * u * u
    square = u * u
    rest = 1.0 - u
    return (
        rest * rest * rest / 6.0,
        (3.0 * cubed - 6.0 * square + 4.0) / 6.0,
        (-3.0 * cubed + 3.0 * square + 3.0 * u + 1.0) / 6.0,
        cubed / 6.0,
    )


def place_rows(start, weights, height, wrap):
    offset = rows_iota((height, A)) - start
    if wrap:
        offset = offset & (wrap - 1)
    result = jnp.zeros((height, A), F32)
    for step in range(4):
        result = jnp.where(offset == step, weights[step], result)
    return result


LOADED = 22


def kernel(
    pos_any, typ_any, snd_any, neigh_any, count_any, cx_any, cy_any, cz_any, frac_any,
    first_any, second_any, third_any, e_in_any, e_hid_any, e_out_any, w_in_any, w_hid_any, w_out_any,
    base_any, table_any, high_any, low_any, twist_any,
    energy_ref, pot_any,
    pos_ref, typ_ref, neigh_ref, count_ref, cx_ref, cy_ref, cz_ref, frac_ref,
    first_ref, second_ref, third_ref, e_in_ref, e_hid_ref, e_out_ref, w_in_ref, w_hid_ref, w_out_ref,
    base_ref, table_ref, high_ref, low_ref, twist_ref,
    low_pos, low_typ, low_snd, upp_pos, upp_typ, upp_snd,
    env_ref, moment_ref, in_h_ref, in_l_ref, desc_h_ref, desc_l_ref, w2_ref, w3_ref,
    charge_ref, charges_ref, wxy_ref, wz_h_ref, wz_l_ref, green_ref,
    out1, in1, out2, in2, out3, in3, out4, in4, modes_ref, pot_ref, part_ref, back_ref,
    load_sem, pot_sem, ghost_send, ghost_recv, cell_send, cell_recv, charge_send, charge_recv,
    part_send, part_recv, send1, recv1, send2, recv2, send3, recv3, send4, recv4,
):
    b = lax.axis_index("brick")
    s = lax.axis_index("slab")
    b_up, b_down = lax.rem(b + 1, NB), lax.rem(b + NB - 1, NB)
    s_up, s_down = lax.rem(s + 1, NS), lax.rem(s + NS - 1, NS)
    below, above = (b_down, s), (b_up, s)
    shifts = ((0, 0), (1, 0), (0, 1), (1, 1))
    onward = ((b, s), (b_up, s), (b, s_up), (b_up, s_up))
    origin = ((b, s), (b_down, s), (b, s_down), (b_down, s_down))

    barrier = pltpu.get_barrier_semaphore()

    def greet_slab(i, carry):
        pl.semaphore_signal(barrier, inc=1, device_id=(b, lax.rem(s + i, NS)), device_id_type=MESH)
        return carry

    def greet_brick(i, carry):
        pl.semaphore_signal(barrier, inc=1, device_id=(lax.rem(b + i, NB), s), device_id_type=MESH)
        return carry

    lax.fori_loop(1, NS, greet_slab, 0)
    lax.fori_loop(1, NB, greet_brick, 0)
    for device in (onward[3], origin[3]):
        pl.semaphore_signal(barrier, inc=1, device_id=device, device_id_type=MESH)

    sources = (
        table_any, first_any, second_any, third_any, w_in_any,
        neigh_any, pos_any, typ_any, count_any, e_in_any,
        e_hid_any, w_hid_any, e_out_any, w_out_any, base_any,
        cx_any, cy_any, cz_any, frac_any, high_any, low_any, twist_any,
    )
    targets = (
        table_ref, first_ref, second_ref, third_ref, w_in_ref,
        neigh_ref, pos_ref, typ_ref, count_ref, e_in_ref,
        e_hid_ref, w_hid_ref, e_out_ref, w_out_ref, base_ref,
        cx_ref.at[0], cy_ref.at[0], cz_ref.at[0], frac_ref.at[0], high_ref, low_ref, twist_ref,
    )
    loads = [
        pltpu.make_async_copy(source, target, load_sem.at[i])
        for i, (source, target) in enumerate(zip(sources, targets, strict=True))
    ]
    for load in loads:
        load.start()

    pl.semaphore_wait(barrier, NS + NB)

    def remote(source, target, send_sem, recv_sem, device):
        return pltpu.make_async_remote_copy(
            src_ref=source, dst_ref=target, send_sem=send_sem, recv_sem=recv_sem,
            device_id=device, device_id_type=MESH,
        )

    plan = (
        (above, pos_any, low_pos), (above, typ_any, low_typ), (above, snd_any, low_snd),
        (below, pos_any, upp_pos), (below, typ_any, upp_typ), (below, snd_any, upp_snd),
    )
    ghosts = [
        remote(source, target, ghost_send.at[i], ghost_recv.at[i], device)
        for i, (device, source, target) in enumerate(plan)
    ]
    for ghost in ghosts:
        ghost.start()
    cells = []
    for n in range(1, 4):
        pairs = ((cx_any, cx_ref), (cy_any, cy_ref), (cz_any, cz_ref), (frac_any, frac_ref))
        for i, (source, target) in enumerate(pairs):
            k = (n - 1) * 4 + i
            cells.append(
                remote(source, target.at[n], cell_send.at[k], cell_recv.at[k], onward[n])
            )
    for cell in cells:
        cell.start()

    row = rows_iota((256, 128))
    lane = lanes_iota((256, 128))

    def kappa(index):
        folded = jnp.minimum(index, NG - index)
        return folded.astype(F32) * (2.0 * math.pi / NG)

    kx = kappa(row // 8 + 32 * (lane // 16))
    ky = kappa(b * 8 + row % 8)
    kz = kappa(s * 16 + lane % 16)
    squared = kx * kx + ky * ky + kz * kz
    root = jnp.where(squared == 0.0, 1.0, 0.0)
    green_ref[...] = (1.0 - root) * jnp.exp(-0.5 * squared) / (squared + root) * (1.0 / NG)

    for load in loads[:4]:
        load.wait()
    f1 = lax.dot_general(table_ref[0:32, 0:25], first_ref[...], NT, precision=HIGHEST)
    oxygen, hydrogen = f1[:, 0:1], f1[:, 1:2]
    w2 = lax.dot_general(table_ref[32:96, 0:50], second_ref[...], NT, precision=HIGHEST)
    w2 = lax.dot_general(w2, table_ref[208:233, 0:96], NN, precision=HIGHEST)
    high, low = halves(w2)
    slot = lanes_iota((64, 96)) // 32
    w2_ref[...] = jnp.where(slot == 1, low.astype(F32), high.astype(F32)).astype(BF16)
    w3 = lax.dot_general(table_ref[96:208, 0:100], third_ref[...], NT, precision=HIGHEST)
    w3 = lax.dot_general(w3, table_ref[240:290, 0:192], NN, precision=HIGHEST)
    high, low = halves(w3)
    slot = lanes_iota((112, 192)) // 64
    w3_ref[...] = jnp.where(slot == 1, low.astype(F32), high.astype(F32)).astype(BF16)

    for load in loads[4:9]:
        load.wait()
    high, low = halves(w_in_ref[...])
    in_h_ref[240:480, :] = high
    in_l_ref[240:480, :] = low

    n = jnp.concatenate(
        [
            neigh_ref[0, :, 0:128],
            jnp.concatenate([neigh_ref[0, 0:32, 128:192], neigh_ref[0, 32:64, 128:192]], axis=1),
        ],
        axis=0,
    )

    def near(row):
        return row[:, 0:128]

    def far(row):
        return jnp.concatenate([row[:, 128:192], row[:, 128:192]], axis=1)

    def by_atom(row):
        return jnp.concatenate(
            [jnp.broadcast_to(near(row), (64, 128)), jnp.broadcast_to(far(row), (32, 128))], axis=0
        )

    own_index = (n - 96) & 127
    lower_index = n & 127
    upper_index = (n - 288) & 127
    row96 = rows_iota((96, 128))
    slot = jnp.where(row96 < 64, row96, row96 - 64 + jnp.where(lanes_iota((96, 128)) < 64, 0, 32))
    live = slot < by_atom(count_ref[...])

    for ghost in ghosts:
        ghost.wait_recv()

    low_snd_row = low_snd[...]
    upp_snd_row = upp_snd[...]
    low_list = jnp.concatenate([low_snd_row[:, 96:192], low_snd_row[:, 0:32]], axis=1)
    upp_list = upp_snd_row[:, 0:128]

    def ghost_row(row, index):
        index = jnp.broadcast_to(index, (8, 128))
        value = jnp.where(index < 128, pick(near(row), index & 127), pick(far(row), index & 127))
        return value[0:1]

    gathered = []
    for c in range(4):
        own = pos_ref[c] if c < 3 else typ_ref[...].astype(F32)
        low = low_pos[c] if c < 3 else low_typ[...].astype(F32)
        upp = upp_pos[c] if c < 3 else upp_typ[...].astype(F32)
        value = jnp.where(n < 224, pick(near(own), own_index), pick(far(own), own_index))
        value = jnp.where(n < 96, pick(ghost_row(low, low_list), lower_index), value)
        value = jnp.where(n >= 288, pick(ghost_row(upp, upp_list), upper_index), value)
        if c < 3:
            value = value - by_atom(own)
        gathered.append(value)
    squared = gathered[0] * gathered[0] + gathered[1] * gathered[1] + gathered[2] * gathered[2]
    smooth = jnp.where(live, 1.0 / (1.0 + squared), 0.0)
    env_ref[0] = smooth
    for c in range(3):
        env_ref[c + 1] = smooth * gathered[c]
    env_ref[4] = gathered[3]
    moment_ref[...] = jnp.zeros_like(moment_ref)

    oxygen_wide = jnp.broadcast_to(oxygen, (32, 128))
    hydrogen_wide = jnp.broadcast_to(hydrogen, (32, 128))

    def chunk(step, carry):
        at = pl.multiple_of(step * 8, 8)
        tile = step // 8
        first = []
        for r in range(8):
            sm = env_ref[0, pl.ds(at + r, 1), :]
            kind = env_ref[4, pl.ds(at + r, 1), :]
            mixing = jnp.where(kind > 0.5, hydrogen_wide, oxygen_wide)
            first.append(jnp.tanh(sm * mixing))
        first = jnp.concatenate(first, axis=1)
        high, low = halves(first)
        second = dot(w2_ref[...], jnp.concatenate([high, high, low], axis=0))
        second = jnp.tanh(second[:56]) + jnp.concatenate([first[:24], first], axis=0)
        padded = jnp.concatenate([second, jnp.zeros((8, 1024), F32)], axis=0)
        high, low = halves(padded)
        third = dot(w3_ref[...], jnp.concatenate([high, high, low], axis=0))
        third = jnp.tanh(third[:104]) + jnp.concatenate([second[:48], second], axis=0)
        for c in range(4):
            total = None
            for r in range(8):
                part = third[:, r * 128 : (r + 1) * 128] * env_ref[c, pl.ds(at + r, 1), :]
                total = part if total is None else total + part
            moment_ref[tile, c] += total
        return carry

    lax.fori_loop(0, 12, chunk, 0, unroll=4)

    for c in range(4):
        moment_ref[0, c] = moment_ref[0, c] * (1.0 / 64.0)
        value = moment_ref[1, c]
        moment_ref[1, c] = (value + pltpu.roll(value, 64, 1)) * (1.0 / 64.0)
    for tile in range(2):
        factors = [moment_ref[tile, c, 0:16, :] for c in range(4)]
        for m, place in enumerate(places()):
            value = None
            for c in range(4):
                term = moment_ref[tile, c, place : place + 1, :] * factors[c]
                value = term if value is None else value + term
            high, low = halves(value)
            desc_h_ref[m * 16 : m * 16 + 16, tile * 128 : (tile + 1) * 128] = high
            desc_l_ref[m * 16 : m * 16 + 16, tile * 128 : (tile + 1) * 128] = low

    for load in loads[10:]:
        load.wait()

    def network(rows, hid_ref, out_ref):
        weight = in_h_ref[rows, :], in_l_ref[rows, :]
        hidden = jnp.tanh(dot3(weight, (desc_h_ref[...], desc_l_ref[...]))).T
        for layer in range(2):
            hidden = jnp.tanh(dot3(halves(hidden), halves(hid_ref[layer]))) + hidden
        row = jnp.broadcast_to(out_ref[...], (16, 240))
        return dot3(halves(row), halves(hidden), NT)[0:1, 0:A]

    def short_energy():
        loads[9].wait()
        high, low = halves(e_in_ref[...])
        in_h_ref[0:240, :] = high
        in_l_ref[0:240, :] = low
        energy_ref[...] = network(slice(0, 240), e_hid_ref, e_out_ref)

    shift = network(slice(240, 480), w_hid_ref, w_out_ref)
    charge = jnp.where(typ_ref[...] == 1, base_ref[0:1, 1:2], base_ref[0:1, 0:1]) + shift
    charge_ref[...] = charge
    charges = [
        remote(charge_ref, charges_ref.at[n], charge_send.at[n], charge_recv.at[n], onward[n])
        for n in range(1, 4)
    ]
    for copy in reversed(charges):
        copy.start()

    for cell in cells:
        cell.wait_recv()
    grid = None
    for n, (dx, dy) in enumerate(shifts):
        wx = place_rows(cx_ref[n] - dx * CX, spline_rows(frac_ref[n, 0]), CX, 0)
        wy = place_rows(cy_ref[n] - dy * CY, spline_rows(frac_ref[n, 1]), CY, 0)
        high, low = halves(place_rows(cz_ref[n], spline_rows(frac_ref[n, 2]), NG, NG))
        wz_h_ref[n] = high
        wz_l_ref[n] = low
        wxy = jnp.concatenate([wx[x : x + 1] * wy for x in range(CX)], axis=0)
        wxy_ref[n] = wxy
    for n in range(4):
        if n:
            charges[n - 1].wait_recv()
        weighted = wxy_ref[n] * (charges_ref[n] if n else charge)
        part = dot3(halves(weighted), (wz_h_ref[n], wz_l_ref[n]), NT)
        grid = part if grid is None else grid + part

    def table(k, count=1):
        at = slice(k * NG, (k + count) * NG)
        return high_ref[at, :], low_ref[at, :]

    spectrum = dot3(halves(grid), table(0))
    chunk_lane = lanes_iota((CY, 128)) // 16
    for to in range(NS):
        tile, chunk_from = divmod(to, 8)
        out = jnp.zeros((CY, 128), F32)
        for x in range(CX):
            source = spectrum[x * CY : (x + 1) * CY, tile * 128 : (tile + 1) * 128]
            shift_by = 16 * (x - chunk_from) % 128
            if shift_by:
                source = pltpu.roll(source, shift_by, 1)
            out = jnp.where(chunk_lane == x, source, out)
        out1[to] = out

    def exchange(source, target, send_sem, recv_sem, me, peers, device_of, meanwhile=None):
        copies = [
            remote(source.at[k], target.at[me], send_sem.at[k], recv_sem.at[me], device_of(k))
            for k in peers
        ]
        for copy in copies:
            copy.start()
        target[me] = source[me]
        if meanwhile is not None:
            meanwhile()
        for k in peers:
            remote(
                source.at[k], target.at[k], send_sem.at[k], recv_sem.at[k], device_of(k)
            ).wait_recv()
        return copies

    far_first = (4, 5, 3, 6, 2, 7, 1)
    turns = [(1, d) for d in (*far_first, 0)] + [(0, d) for d in far_first]
    slabs = [lax.rem(s // 8 + half, 2) * 8 + lax.rem(s + d, 8) for half, d in turns]
    turns = [(x, d) for x in (2, 1, 3) for d in (*far_first, 0)] + [(0, d) for d in far_first]
    bricks = [lax.rem(b // 8 + x, 4) * 8 + lax.rem(b + d, 8) for x, d in turns]

    def over_slab(source, target, send_sem, recv_sem, meanwhile=None):
        return exchange(
            source, target, send_sem, recv_sem, s, slabs, lambda to: (b, to), meanwhile
        )

    def over_brick(source, target, send_sem, recv_sem):
        return exchange(source, target, send_sem, recv_sem, b, bricks, lambda to: (to, s))

    sent = over_slab(out1, in1, send1, recv1, short_energy)
    data = halves(in1[...].reshape(NG, 128))
    out2[...] = dot3_narrow(table(1), data).reshape(NB, 8, 128)
    sent += over_brick(out2, in2, send2, recv2)

    data = halves(in2[...].reshape(NG, 128))
    both = dot3_narrow(table(2, 2), data)
    uc, us = both[:256], both[256:]
    tc, ts = twist_ref[0:256, :], twist_ref[256:512, :]
    turned = jnp.concatenate([uc * tc - us * ts, -(uc * ts + us * tc)], axis=1)
    green = green_ref[...]
    modes = dot3(halves(turned), table(4)) * jnp.concatenate([green, green], axis=1)
    back = dot3(halves(modes), table(4), NT)
    vr, vi = back[:, :128], back[:, 128:]
    real = dot3_narrow(table(2), halves(vr * tc - vi * ts))
    imag = dot3_narrow(table(3), halves(vr * ts + vi * tc))
    out3[...] = (real - imag).reshape(NB, 8, 128)
    sent += over_brick(out3, in3, send3, recv3)
    data = halves(in3[...].reshape(NG, 128))
    out4[...] = dot3_narrow(table(0), data).reshape(NS, CY, 128)
    sent += over_slab(out4, in4, send4, recv4)

    for x in range(CX):
        for tile in range(2):
            out = jnp.zeros((CY, 128), F32)
            for c in range(8):
                source = in4[8 * tile + c]
                shift_by = 16 * (c - x) % 128
                if shift_by:
                    source = pltpu.roll(source, shift_by, 1)
                out = jnp.where(chunk_lane == c, source, out)
            modes_ref[x * CY : (x + 1) * CY, tile * 128 : (tile + 1) * 128] = out
    potential = dot3(halves(modes_ref[...]), table(0), NT)
    pot_ref[...] = potential.reshape(CX, CY, NG)
    pot_copy = pltpu.make_async_copy(pot_ref, pot_any, pot_sem)
    pot_copy.start()

    data = halves(potential)
    returns = []
    for n in (3, 1, 2, 0):
        sampled = dot3(data, (wz_h_ref[n], wz_l_ref[n]))
        part_ref[n] = jnp.sum(sampled * wxy_ref[n], axis=0, keepdims=True)
        if n:
            copy = remote(part_ref.at[n], back_ref.at[n], part_send.at[n], part_recv.at[n], origin[n])
            copy.start()
            returns.append(copy)
    for copy in sent + ghosts + cells + charges:
        copy.wait_send()
    for copy in returns:
        copy.wait_recv()
    at = part_ref[0] + back_ref[1] + back_ref[2] + back_ref[3]
    energy_ref[...] += 0.5 * charge_ref[...] * at
    for copy in returns:
        copy.wait_send()
    pot_copy.wait()


def hand_over(energy_in, pot_in, energy_out, pot_out, energy_ref, pot_ref, sem):
    arriving = [
        pltpu.make_async_copy(energy_in, energy_ref, sem.at[0]),
        pltpu.make_async_copy(pot_in, pot_ref, sem.at[1]),
    ]
    leaving = [
        pltpu.make_async_copy(energy_ref, energy_out, sem.at[2]),
        pltpu.make_async_copy(pot_ref, pot_out, sem.at[3]),
    ]
    for copy in arriving:
        copy.start()
    for first, second in zip(arriving, leaving, strict=True):
        first.wait()
        second.start()
    for copy in leaving:
        copy.wait()


VMEM = pl.BlockSpec(memory_space=pltpu.VMEM)
ANY = pl.BlockSpec(memory_space=pl.ANY)
I32 = jnp.int32


def per_device(
    positions, types, neighbours, neighbour_count, send_index, cell_x, cell_y, cell_z, spline_fraction,
    embed_first, embed_second, embed_third, energy_in, energy_hidden, energy_out,
    wannier_in, wannier_hidden, wannier_out, charge_base,
):
    vmem = pltpu.VMEM
    dma = pltpu.SemaphoreType.DMA
    slab_block, brick_block = vmem((NS, CY, 128), F32), vmem((NB, 8, 128), F32)
    outs = (jax.ShapeDtypeStruct((1, A), F32), jax.ShapeDtypeStruct((CX, CY, NG), F32))
    results = tuple(
        pl.pallas_call(
            kernel,
            out_shape=outs,
            in_specs=[ANY] * 23,
            out_specs=(VMEM, ANY),
            scratch_shapes=[
                vmem((3, 1, A), F32), vmem((1, A), I32), vmem((1, 64, A), I32), vmem((1, A), I32),
                vmem((4, 1, A), I32), vmem((4, 1, A), I32), vmem((4, 1, A), I32), vmem((4, 3, 1, A), F32),
                vmem((2, 25), F32), vmem((25, 50), F32), vmem((50, 100), F32),
                vmem((240, 1600), F32), vmem((2, 240, 240), F32), vmem((1, 240), F32),
                vmem((240, 1600), F32), vmem((2, 240, 240), F32), vmem((1, 240), F32),
                vmem((1, 2), F32), vmem((296, 256), F32),
                vmem((5 * NG, NG), BF16), vmem((5 * NG, NG), BF16), vmem((2 * NG, 128), F32),
                vmem((3, 1, A), F32), vmem((1, A), I32), vmem((1, A), I32),
                vmem((3, 1, A), F32), vmem((1, A), I32), vmem((1, A), I32),
                vmem((5, 96, 128), F32), vmem((2, 4, 104, 128), F32),
                vmem((480, 1600), BF16), vmem((480, 1600), BF16),
                vmem((1600, 256), BF16), vmem((1600, 256), BF16),
                vmem((64, 96), BF16), vmem((112, 192), BF16),
                vmem((1, A), F32), vmem((4, 1, A), F32), vmem((4, 128, A), F32),
                vmem((4, NG, A), BF16), vmem((4, NG, A), BF16), vmem((NG, 128), F32),
                slab_block, slab_block, brick_block, brick_block,
                brick_block, brick_block, slab_block, slab_block,
                vmem((128, NG), F32), vmem((CX, CY, NG), F32), vmem((4, 1, A), F32), vmem((4, 1, A), F32),
                dma((LOADED,)), dma, dma((6,)), dma((6,)), dma((12,)), dma((12,)), dma((4,)), dma((4,)),
                dma((4,)), dma((4,)), dma((NS,)), dma((NS,)), dma((NB,)), dma((NB,)),
                dma((NB,)), dma((NB,)), dma((NS,)), dma((NS,)),
            ],
            compiler_params=pltpu.CompilerParams(
                collective_id=1, has_side_effects=True, vmem_limit_bytes=60 * MIB
            ),
            name="potential",
        )(
            positions, types, send_index, jnp.swapaxes(neighbours, 1, 2), neighbour_count,
            cell_x, cell_y, cell_z, spline_fraction,
            embed_first, embed_second, embed_third,
            energy_in.T, energy_hidden, energy_out.reshape(1, -1),
            wannier_in.T, wannier_hidden, wannier_out.reshape(1, -1), charge_base.reshape(1, 2),
            embedding_tables(), *transform_tables(),
        )
    )
    return pl.pallas_call(
        hand_over,
        out_shape=outs,
        in_specs=[ANY, ANY],
        out_specs=(ANY, ANY),
        scratch_shapes=[vmem((1, A), F32), vmem((CX, CY, NG), F32), dma((4,))],
        compiler_params=pltpu.CompilerParams(vmem_limit_bytes=60 * MIB),
        name="hand_over",
    )(*results)


def solution(mesh):
    row = P("slab", "brick")
    three = P(None, "slab", "brick")
    placed = (three, row, P("slab", "brick", None), row, row, row, row, row, three) + (P(),) * 10
    return jax.shard_map(
        per_device,
        mesh=mesh,
        in_specs=placed,
        out_specs=(row, P("brick", "slab", None)),
        check_vma=False,
    )
```
